512 devices in a mesh: dp: 32 (over y_lo, x, core), tensor: 16 (over z, y_hi).
Axes of the slice: x: 4, y: 8 (y_hi: 2, y_lo: 4; y = y_hi * 4 + y_lo), z: 8, core: 2. Of those that a mesh axis runs over, the one named last changes fastest.
Arguments:
- norm_input: bfloat16 [65536, 8192], P(('dp', 'tensor')), may hold values from -6 to 6
- key_grad: bfloat16 [65536, 512], P(('dp', 'tensor')), may hold values from -100 to 100
- positions: int32 [65536], P(('dp', 'tensor')), may hold values from 0 to 8191
- norm_gain: bfloat16 [8192], replicated, may hold values from 0.25 to 1.75
- key_weight: bfloat16 [512, 8192], P('dp', 'tensor'), may hold values from -0.0625 to 0.0625
- first_moment: float32 [512, 8192], P('dp', 'tensor'), may hold values from -6 to 6
- second_moment: float32 [512, 8192], P('dp', 'tensor'), may hold values from 0.1 to 4
Outputs:
- input_grad: bfloat16 [65536, 8192], P(('dp', 'tensor'))
- new_weight: bfloat16 [512, 8192], P(None, 'tensor')
- new_first: float32 [512, 8192], P('dp', 'tensor')
- new_second: float32 [512, 8192], P('dp', 'tensor')
The draws below stay inside these ranges and needn't reach their ends.
All inputs are finite; a program needn't handle non-finite values.
Results may differ from the reference program's by a relative error of at most 0.01.
Values may be sent and summed in bfloat16 or wider, within the bound.
No kernel may reach another device: no remote copies, remote signals or barrier semaphores. Data moves between devices by JAX's collectives and lax.ppermute only.
A program may use at most 64 MiB of HBM per device.

```python
import math
import jax
import jax.numpy as jnp
from jax import lax

D = 8192
KV_HEADS = 4
HEAD = 128
TOK_DEV = 2048
KV = 512
TOKENS = 65536
N_DP = 32


def draw_key_grad(key, part):
    key_base = jax.random.fold_in(key, 11)
    key_column = jax.random.fold_in(key, 12)
    column_rise = jnp.arange(KV, dtype=jnp.float32) / KV
    column_jitter = jax.random.uniform(key_column, (KV,), jnp.float32, 0.0, 0.3)
    column_scale = 0.3 * 10.0 ** (column_rise + column_jitter)
    values = jax.random.truncated_normal(key_base, -4.0, 4.0, (TOKENS, KV), jnp.float32) * column_scale[None, :]
    return values.astype(jnp.bfloat16)


def set_ends(values, rng, smallest, top_value):
    longest = values.shape.index(max(values.shape))
    spots = []
    for shift in (0, 1):
        where = [jax.random.randint(jax.random.fold_in(rng, axis), (), 0, length) for axis, length in enumerate(values.shape)]
        where[longest] = (where[longest] + shift) % values.shape[longest]
        spots.append(tuple(where))
    return values.at[spots[0]].set(smallest).at[spots[1]].set(top_value)


def shard_levels(stream_key, extent, split, least, top_value):
    gain = 1.0
    for dim, blocks in split:
        steps = jax.random.uniform(jax.random.fold_in(jax.random.fold_in(stream_key, 6), dim), (blocks,), jnp.float32, least / len(split), top_value / len(split))
        gain = gain * jnp.repeat(jnp.exp(steps), extent[dim] // blocks).reshape((-1,) + (1,) * (len(extent) - 1 - dim))
    return gain


def centred(stream_key, extent, scale, reach, split=(), kind=jnp.bfloat16):
    drawn = scale * jax.random.normal(stream_key, extent, jnp.float32)
    if split:
        drawn = drawn * shard_levels(stream_key, extent, split, -0.22, 0.18)
    return jnp.clip(drawn, -reach, reach).astype(kind)


def setup_inputs(seed: int = 0) -> dict:
    splits = jax.random.split(jax.random.key(seed), 8)
    norm_input = centred(splits[0], (TOKENS, D), 1.0, 6.0, ((0, 512),))
    key_grad = draw_key_grad(jax.random.fold_in(splits[7], 71), 0)
    positions = set_ends(jax.random.randint(splits[2], (TOKENS,), 0, 8192), jax.random.fold_in(splits[2], 1), 0, 8191).astype(jnp.int32)
    norm_gain = jnp.clip(1.0 + 0.15 * jax.random.normal(splits[3], (D,), jnp.float32), 0.25, 1.75).astype(jnp.bfloat16)
    key_weight = centred(splits[4], (KV, D), D ** -0.5, 0.0625, ((0, 32), (1, 16)))
    first_moment = centred(splits[5], (KV, D), 1.0, 6.0, ((0, 32), (1, 16)), jnp.float32)
    second_moment = jnp.clip(jnp.exp(math.log(4.0) - 3.6888794 * jax.random.uniform(splits[6], (KV, D), jnp.float32) ** shard_levels(splits[6], (KV, D), ((0, 32), (1, 16)), -0.2, 0.2)), 0.1, 4.0)
    return {"norm_input": norm_input, "key_grad": key_grad, "positions": positions, "norm_gain": norm_gain, "key_weight": key_weight, "first_moment": first_moment, "second_moment": second_moment}


eps_norm = 1e-05
beta_one = 0.9
beta_two = 0.95
learn_rate = 0.0003
decay_rate = 0.1
eps_adam = 1e-08

def unrotate(incoming, positions):
    row_count = incoming.shape[0]
    half_width = HEAD // 2
    frequency = 500000.0 ** (-(2.0 * jnp.arange(half_width, dtype=jnp.float32)) / HEAD)
    angles = positions.astype(jnp.float32)[:, None] * frequency[None, :]
    cosine = jnp.cos(angles)[:, None, :]
    sine_table = jnp.sin(angles)[:, None, :]
    pieces = incoming.astype(jnp.float32).reshape(row_count, KV_HEADS, 2, half_width)
    first_half = pieces[:, :, 0, :]
    second_half = pieces[:, :, 1, :]
    upper_part = first_half * cosine + second_half * sine_table
    lower_part = second_half * cosine - first_half * sine_table
    return jnp.stack([upper_part, lower_part], axis=2).reshape(row_count, KV).astype(jnp.bfloat16)

def reference(norm_input, key_grad, positions, norm_gain, key_weight, first_moment, second_moment):
    gain_f32 = norm_gain.astype(jnp.float32)
    key_back = unrotate(key_grad, positions)
    inputs = norm_input.reshape(N_DP, TOK_DEV, D)
    cotangents = key_back.reshape(N_DP, TOK_DEV, KV)

    def one_group(total, group):
        inputs_g, keys_g = group
        inputs_f32 = inputs_g.astype(jnp.float32)
        scale_inv = lax.rsqrt(lax.optimization_barrier(jnp.mean(inputs_f32 * inputs_f32, axis=1, keepdims=True)) + eps_norm)
        normalized = inputs_f32 * scale_inv
        normed = (normalized * gain_f32).astype(jnp.bfloat16)
        upstream = jnp.dot(keys_g, key_weight, preferred_element_type=jnp.float32)
        weighted = upstream * gain_f32
        inner = lax.optimization_barrier(jnp.mean(weighted * normalized, axis=1, keepdims=True))
        group_grad = (scale_inv * (weighted - normalized * inner)).astype(jnp.bfloat16)
        partial_sum = lax.dot_general(keys_g, normed, (((0,), (0,)), ((), ())), preferred_element_type=jnp.float32)
        rounded = lax.optimization_barrier(partial_sum.astype(jnp.bfloat16))
        return (total + rounded.astype(jnp.float32), group_grad)
    weight_grad, grads = lax.scan(one_group, jnp.zeros((KV, D), jnp.float32), (inputs, cotangents))
    input_grad = grads.reshape(TOKENS, D)
    clip_limit = math.sqrt(KV * D)
    grad_size = jnp.sqrt(jnp.sum(weight_grad * weight_grad))
    clip_factor = jnp.minimum(1.0, clip_limit / (grad_size + 1e-06))
    clipped = weight_grad * clip_factor
    new_first = beta_one * first_moment + (1.0 - beta_one) * clipped
    new_second = beta_two * second_moment + (1.0 - beta_two) * clipped * clipped
    weight_f32 = key_weight.astype(jnp.float32)
    new_weight = (weight_f32 * (1.0 - learn_rate * decay_rate) - learn_rate * new_first / (jnp.sqrt(new_second) + eps_adam)).astype(jnp.bfloat16)
    return (input_grad, new_weight, new_first, new_second)
```

```python
import math

import jax
import jax.numpy as jnp
from jax import lax
from jax.experimental import pallas as pl
from jax.experimental.pallas import tpu as pltpu
from jax.sharding import Mesh
from jax.sharding import PartitionSpec as P

D = 8192
KV_HEADS = 4
HEAD = 128
KV = KV_HEADS * HEAD
DP = ("yl", "x", "c")
TENSOR = ("z", "yh")
DP_TENSOR = DP + TENSOR
GROUP = ("x", "c")
PLANE = ("yl", "z", "yh")
N_GROUP = 8
N_PLANE = 64
WIDE = D // N_GROUP
COLS = WIDE + KV

eps_norm = 1e-05
beta_one = 0.9
beta_two = 0.95
learn_rate = 0.0003
decay_rate = 0.1
eps_adam = 1e-08

bf16 = jnp.bfloat16
f32 = jnp.float32


def exchange(x, axes):
    return lax.all_to_all(x, axes, split_axis=0, concat_axis=0, tiled=True)


def copies_for(x, count):
    return jnp.broadcast_to(x, (count, *x.shape))


def sum_over(x, axes, count):
    return jnp.sum(exchange(copies_for(x, count), axes), axis=0)


def rotation(positions):
    half_width = HEAD // 2
    frequency = 500000.0 ** (-(2.0 * jnp.arange(half_width, dtype=f32)) / HEAD)
    angles = positions.astype(f32)[:, None] * frequency[None, :]
    cosine = jnp.cos(angles)
    sine = jnp.sin(angles)
    return jnp.concatenate([cosine, cosine], axis=1), jnp.concatenate([sine, -sine], axis=1)


def prepare_kernel(x_ref, key_ref, cos_ref, sin_ref, gain_ref, send_ref, key_out_ref, scale_ref):
    x = x_ref[...].astype(f32)
    scale = lax.rsqrt(jnp.sum(x * x, axis=1, keepdims=True) / D + eps_norm)
    scale_ref[...] = jnp.broadcast_to(scale, scale_ref.shape)
    normed = (x * scale * gain_ref[...]).astype(bf16)
    for j in range(N_GROUP):
        send_ref[j, :, :WIDE] = normed[:, j * WIDE : (j + 1) * WIDE]
    for h in range(KV_HEADS):
        part = key_ref[:, h * HEAD : (h + 1) * HEAD].astype(f32)
        turned = part * cos_ref[...] + pltpu.roll(part, HEAD // 2, 1) * sin_ref[...]
        turned = turned.astype(bf16)
        key_out_ref[:, h * HEAD : (h + 1) * HEAD] = turned
        for j in range(N_GROUP):
            send_ref[j, :, WIDE + h * HEAD : WIDE + (h + 1) * HEAD] = turned


def prepare(x, key_grad, cosine, sine, gain):
    tokens = x.shape[0]
    tile = 32
    return pl.pallas_call(
        prepare_kernel,
        grid=(tokens // tile,),
        in_specs=[
            pl.BlockSpec((tile, D), lambda i: (i, 0)),
            pl.BlockSpec((tile, KV), lambda i: (i, 0)),
            pl.BlockSpec((tile, HEAD), lambda i: (i, 0)),
            pl.BlockSpec((tile, HEAD), lambda i: (i, 0)),
            pl.BlockSpec((1, D), lambda i: (0, 0)),
        ],
        out_specs=[
            pl.BlockSpec((N_GROUP, tile, COLS), lambda i: (0, i, 0)),
            pl.BlockSpec((tile, KV), lambda i: (i, 0)),
            pl.BlockSpec((tile, HEAD), lambda i: (i, 0)),
        ],
        out_shape=[
            jax.ShapeDtypeStruct((N_GROUP, tokens, COLS), bf16),
            jax.ShapeDtypeStruct((tokens, KV), bf16),
            jax.ShapeDtypeStruct((tokens, HEAD), f32),
        ],
        compiler_params=pltpu.CompilerParams(vmem_limit_bytes=56 * 1024 * 1024),
        cost_estimate=pl.CostEstimate(flops=8 * tokens * D, bytes_accessed=6 * 1024 * 1024, transcendentals=0),
    )(x, key_grad, cosine, sine, gain)


def product_kernel(key_ref, normed_ref, out_ref):
    tokens = key_ref.shape[0] * key_ref.shape[1]
    keys = key_ref[...].reshape(tokens, KV)
    normed = normed_ref[...].reshape(tokens, normed_ref.shape[2])
    total = lax.dot_general(keys, normed, (((0,), (0,)), ((), ())), preferred_element_type=f32)
    out_ref[...] = total.astype(bf16).reshape(out_ref.shape)


def product(received):
    count, tokens, _ = received.shape
    half = WIDE // 2
    return pl.pallas_call(
        product_kernel,
        grid=(2,),
        in_specs=[
            pl.BlockSpec((count, tokens, KV), lambda h: (0, 0, WIDE // KV)),
            pl.BlockSpec((count, tokens, half), lambda h: (0, 0, h)),
        ],
        out_specs=pl.BlockSpec((32, 1, 16, half), lambda h: (0, h, 0, 0)),
        out_shape=jax.ShapeDtypeStruct((32, 2, 16, half), bf16),
        compiler_params=pltpu.CompilerParams(vmem_limit_bytes=32 * 1024 * 1024),
        cost_estimate=pl.CostEstimate(
            flops=2 * count * tokens * KV * WIDE, bytes_accessed=4 * 1024 * 1024, transcendentals=0
        ),
    )(received, received)


def backward_kernel(core_ref, key_ref, own_ref, other_ref, x_ref, scale_ref, gain_ref, out_ref, held, cross):
    step = pl.program_id(0)
    core = core_ref[0]
    tokens = key_ref.shape[0]
    half = own_ref.shape[4]

    @pl.when(step == 0)
    def _():
        cross[...] = jnp.zeros_like(cross)

    for side, ref in ((core, own_ref), (1 - core, other_ref)):
        inside = pl.ds(pl.multiple_of(side * half, half), half)
        columns = pl.ds(pl.multiple_of(step * 2 * half + side * half, half), half)
        up = jnp.dot(key_ref[...], ref[...].reshape(KV, half), preferred_element_type=f32)
        weighted = up * gain_ref[:, inside]
        held[step, :, inside] = weighted
        term = jnp.sum(weighted * x_ref[:, columns].astype(f32), axis=1, keepdims=True)
        cross[...] += jnp.broadcast_to(term, (tokens, HEAD))

    @pl.when(step == pl.num_programs(0) - 1)
    def _():
        scale = scale_ref[:, :1]
        inner = scale * (cross[:, :1] / D)
        width = 2 * half
        for t in range(D // width):
            part = slice(t * width, (t + 1) * width)
            xhat = x_ref[:, part].astype(f32) * scale
            out_ref[:, part] = (scale * (held[t] - xhat * inner)).astype(bf16)


def backward(core, keys, own, other, x, scale, gain):
    tokens = x.shape[0]
    width = 512
    steps = D // width
    weights = pl.BlockSpec((1, 4, 1, 128, width // 2), lambda t, core: (t % 2, 0, t // 2, 0, 0))
    whole = lambda a: pl.BlockSpec(a.shape, lambda t, core: (0, 0))
    return pl.pallas_call(
        backward_kernel,
        grid_spec=pltpu.PrefetchScalarGridSpec(
            num_scalar_prefetch=1,
            grid=(steps,),
            in_specs=[
                whole(keys),
                weights,
                weights,
                whole(x),
                whole(scale),
                pl.BlockSpec((1, width), lambda t, core: (0, t)),
            ],
            out_specs=pl.BlockSpec((tokens, D), lambda t, core: (0, 0)),
            scratch_shapes=[pltpu.VMEM((steps, tokens, width), f32), pltpu.VMEM((tokens, HEAD), f32)],
        ),
        out_shape=jax.ShapeDtypeStruct((tokens, D), bf16),
        compiler_params=pltpu.CompilerParams(vmem_limit_bytes=56 * 1024 * 1024),
        cost_estimate=pl.CostEstimate(
            flops=2 * tokens * KV * D, bytes_accessed=12 * 1024 * 1024, transcendentals=0
        ),
    )(core, keys, own, other, x, scale, gain)


def weights_of_core(key_weight):
    rows, columns = key_weight.shape
    halves = key_weight.reshape(rows, 2, columns // 2).transpose(1, 0, 2)
    send = jnp.broadcast_to(halves, (4, *halves.shape)).reshape(N_GROUP, rows, columns // 2)
    pieces = exchange(send, GROUP).reshape(N_GROUP * rows, columns // 2)
    whole = lax.all_gather(pieces, ("yh", "yl", "z"), axis=0, tiled=True)
    return whole.reshape(2, 4, 8, *pieces.shape)


def body(norm_input, key_grad, positions, norm_gain, key_weight, first_moment, second_moment):
    gain = norm_gain.astype(f32)[None, :]
    core = lax.axis_index("c").astype(jnp.int32).reshape(1)
    own = weights_of_core(key_weight)
    cosine, sine = rotation(positions)
    send, keys, scale = prepare(norm_input, key_grad, cosine, sine, gain)
    received = exchange(send, GROUP)
    partial = product(received).reshape(N_PLANE, 16, 512)
    pieces = exchange(partial, PLANE)
    piece = jnp.sum(pieces.astype(f32), axis=0)
    own, _ = lax.optimization_barrier((own, piece))
    other = lax.ppermute(own, "c", [(0, 1), (1, 0)])

    swap = [(i * 8 + k, k * 8 + i) for i in range(8) for k in range(8)]
    grad_shard = lax.ppermute(piece, ("x", "c", "z"), swap)
    square = jnp.broadcast_to(jnp.sum(piece * piece), (8, 128))
    square = sum_over(square, GROUP, 8)
    square = sum_over(square, ("yh", "yl"), 8)
    square = sum_over(square, "z", 8)
    total_square = square[0, 0]

    clip_limit = math.sqrt(KV * D)
    clip_factor = jnp.minimum(1.0, clip_limit / (jnp.sqrt(total_square) + 1e-06))
    clipped = grad_shard * clip_factor
    new_first = beta_one * first_moment + (1.0 - beta_one) * clipped
    new_second = beta_two * second_moment + (1.0 - beta_two) * clipped * clipped
    own_rows = key_weight.astype(f32)
    updated = (
        own_rows * (1.0 - learn_rate * decay_rate)
        - learn_rate * new_first / (jnp.sqrt(new_second) + eps_adam)
    ).astype(bf16)
    new_weight = exchange(copies_for(updated, 32), DP).reshape(KV, 512)

    input_grad = backward(core, keys, own, other, norm_input, scale, gain)
    return (input_grad, new_weight, new_first, new_second)


def solution(mesh):
    split = Mesh(mesh.devices.reshape(4, 4, 2, 8, 2), ("yl", "x", "c", "z", "yh"))
    placed = (
        P(DP_TENSOR, None),
        P(DP_TENSOR, None),
        P(DP_TENSOR),
        P(),
        P(DP, TENSOR),
        P(DP, TENSOR),
        P(DP, TENSOR),
    )
    return jax.shard_map(
        body,
        mesh=split,
        in_specs=placed,
        out_specs=(P(DP_TENSOR, None), P(None, TENSOR), P(DP, TENSOR), P(DP, TENSOR)),
        check_vma=False,
    )
```

```python
import math

import jax
import jax.numpy as jnp
from jax import lax
from jax.experimental import pallas as pl
from jax.experimental.pallas import tpu as pltpu
from jax.sharding import Mesh
from jax.sharding import PartitionSpec as P

D = 8192
KV_HEADS = 4
HEAD = 128
KV = KV_HEADS * HEAD
DP = ("yl", "x", "c")
TENSOR = ("z", "yh")
DP_TENSOR = DP + TENSOR
GROUP = ("x", "c")
PLANE = ("yl", "z", "yh")
N_GROUP = 8
N_PLANE = 64
WIDE = D // N_GROUP
COLS = WIDE + KV

eps_norm = 1e-05
beta_one = 0.9
beta_two = 0.95
learn_rate = 0.0003
decay_rate = 0.1
eps_adam = 1e-08

bf16 = jnp.bfloat16
f32 = jnp.float32


def exchange(x, axes):
    return lax.all_to_all(x, axes, split_axis=0, concat_axis=0, tiled=True)


def copies_for(x, count):
    return jnp.broadcast_to(x, (count, *x.shape))


def rotation(positions):
    half_width = HEAD // 2
    frequency = 500000.0 ** (-(2.0 * jnp.arange(half_width, dtype=f32)) / HEAD)
    angles = positions.astype(f32)[:, None] * frequency[None, :]
    cosine = jnp.cos(angles)
    sine = jnp.sin(angles)
    return jnp.concatenate([cosine, cosine], axis=1), jnp.concatenate([sine, -sine], axis=1)


def prepare_kernel(x_ref, key_ref, cos_ref, sin_ref, gain_ref, send_ref, key_out_ref, scale_ref):
    x = x_ref[...].astype(f32)
    scale = lax.rsqrt(jnp.sum(x * x, axis=1, keepdims=True) / D + eps_norm)
    scale_ref[...] = jnp.broadcast_to(scale, scale_ref.shape)
    normed = (x * scale * gain_ref[...].astype(f32)).astype(bf16)
    for j in range(N_GROUP):
        send_ref[j, :, :WIDE] = normed[:, j * WIDE : (j + 1) * WIDE]
    for h in range(KV_HEADS):
        part = key_ref[:, h * HEAD : (h + 1) * HEAD].astype(f32)
        turned = part * cos_ref[...] + pltpu.roll(part, HEAD // 2, 1) * sin_ref[...]
        turned = turned.astype(bf16)
        key_out_ref[:, h * HEAD : (h + 1) * HEAD] = turned
        for j in range(N_GROUP):
            send_ref[j, :, WIDE + h * HEAD : WIDE + (h + 1) * HEAD] = turned


def prepare(x, key_grad, cosine, sine, gain):
    tokens = x.shape[0]
    tile = 32
    return pl.pallas_call(
        prepare_kernel,
        grid=(tokens // tile,),
        in_specs=[
            pl.BlockSpec((tile, D), lambda i: (i, 0)),
            pl.BlockSpec((tile, KV), lambda i: (i, 0)),
            pl.BlockSpec((tile, HEAD), lambda i: (i, 0)),
            pl.BlockSpec((tile, HEAD), lambda i: (i, 0)),
            pl.BlockSpec((1, D), lambda i: (0, 0)),
        ],
        out_specs=[
            pl.BlockSpec((N_GROUP, tile, COLS), lambda i: (0, i, 0)),
            pl.BlockSpec((tile, KV), lambda i: (i, 0)),
            pl.BlockSpec((tile, HEAD), lambda i: (i, 0)),
        ],
        out_shape=[
            jax.ShapeDtypeStruct((N_GROUP, tokens, COLS), bf16),
            jax.ShapeDtypeStruct((tokens, KV), bf16),
            jax.ShapeDtypeStruct((tokens, HEAD), f32),
        ],
        compiler_params=pltpu.CompilerParams(vmem_limit_bytes=56 * 1024 * 1024),
        cost_estimate=pl.CostEstimate(flops=8 * tokens * D, bytes_accessed=6 * 1024 * 1024, transcendentals=0),
    )(x, key_grad, cosine, sine, gain)


def product_kernel(key_ref, normed_ref, out_ref):
    tokens = key_ref.shape[0] * key_ref.shape[1]
    keys = key_ref[...].reshape(tokens, KV)
    normed = normed_ref[...].reshape(tokens, normed_ref.shape[2])
    total = lax.dot_general(keys, normed, (((0,), (0,)), ((), ())), preferred_element_type=f32)
    out_ref[...] = total.astype(bf16).reshape(out_ref.shape)


def product(received):
    count, tokens, _ = received.shape
    half = WIDE // 2
    return pl.pallas_call(
        product_kernel,
        grid=(2,),
        in_specs=[
            pl.BlockSpec((count, tokens, KV), lambda h: (0, 0, WIDE // KV)),
            pl.BlockSpec((count, tokens, half), lambda h: (0, 0, h)),
        ],
        out_specs=pl.BlockSpec((32, 1, 16, half), lambda h: (0, h, 0, 0)),
        out_shape=jax.ShapeDtypeStruct((32, 2, 16, half), bf16),
        compiler_params=pltpu.CompilerParams(vmem_limit_bytes=32 * 1024 * 1024),
        cost_estimate=pl.CostEstimate(
            flops=2 * count * tokens * KV * WIDE, bytes_accessed=4 * 1024 * 1024, transcendentals=0
        ),
    )(received, received)


def backward_kernel(core_ref, key_ref, own_ref, other_ref, x_ref, scale_ref, gain_ref, out_ref, held, cross):
    step = pl.program_id(0)
    core = core_ref[0]
    tokens = key_ref.shape[0]
    half = own_ref.shape[4]
    width = 2 * half
    first = step * own_ref.shape[2] * 2

    @pl.when(step == 0)
    def _():
        cross[...] = jnp.zeros_like(cross)

    total = jnp.zeros(cross.shape, f32)
    for z in range(own_ref.shape[2]):
        for yh in range(2):
            block = z * 2 + yh
            for side, ref in ((core, own_ref), (1 - core, other_ref)):
                inside = pl.ds(pl.multiple_of(side * half, half), half)
                columns = pl.ds(pl.multiple_of((first + block) * width + side * half, half), half)
                local = pl.ds(pl.multiple_of(block * width + side * half, half), half)
                up = jnp.dot(key_ref[...], ref[yh, :, z].reshape(KV, half), preferred_element_type=f32)
                weighted = up * gain_ref[:, local].astype(f32)
                held[first + block, :, inside] = weighted
                term = weighted * x_ref[:, columns].astype(f32)
                for k in range(half // HEAD):
                    total += term[:, k * HEAD : (k + 1) * HEAD]
    cross[...] += total

    @pl.when(step == pl.num_programs(0) - 1)
    def _():
        scale = scale_ref[:, :1]
        inner = scale * scale * (jnp.sum(cross[...], axis=1, keepdims=True) / D)
        for t in range(D // width):
            part = slice(t * width, (t + 1) * width)
            x = x_ref[:, part].astype(f32)
            out_ref[:, part] = (scale * (held[t] - x * inner)).astype(bf16)


def backward(core, keys, own, other, x, scale, gain):
    tokens = x.shape[0]
    width = 512
    deep = 2
    steps = 8 // deep
    weights = pl.BlockSpec((2, 4, deep, 128, width // 2), lambda t, core: (0, 0, t, 0, 0))
    whole = lambda a: pl.BlockSpec(a.shape, lambda t, core: (0, 0))
    return pl.pallas_call(
        backward_kernel,
        grid_spec=pltpu.PrefetchScalarGridSpec(
            num_scalar_prefetch=1,
            grid=(steps,),
            in_specs=[
                whole(keys),
                weights,
                weights,
                whole(x),
                whole(scale),
                pl.BlockSpec((1, 2 * deep * width), lambda t, core: (0, t)),
            ],
            out_specs=pl.BlockSpec((tokens, D), lambda t, core: (0, 0)),
            scratch_shapes=[pltpu.VMEM((D // width, tokens, width), f32), pltpu.VMEM((tokens, HEAD), f32)],
        ),
        out_shape=jax.ShapeDtypeStruct((tokens, D), bf16),
        compiler_params=pltpu.CompilerParams(vmem_limit_bytes=56 * 1024 * 1024),
        cost_estimate=pl.CostEstimate(
            flops=2 * tokens * KV * D, bytes_accessed=12 * 1024 * 1024, transcendentals=0
        ),
    )(core, keys, own, other, x, scale, gain)


def local_call(kernel, outs, *args):
    return pl.pallas_call(
        kernel,
        out_shape=[jax.ShapeDtypeStruct(shape, kind) for shape, kind in outs],
        compiler_params=pltpu.CompilerParams(vmem_limit_bytes=32 * 1024 * 1024),
    )(*args)


def add_pieces_kernel(pieces_ref, piece_ref, square_ref):
    piece = jnp.sum(pieces_ref[...].astype(f32), axis=0)
    piece_ref[...] = piece
    square = jnp.sum(jnp.sum(piece * piece, axis=0, keepdims=True), axis=1, keepdims=True)
    square_ref[...] = jnp.broadcast_to(square, square_ref.shape)


def add_pieces(pieces):
    return local_call(add_pieces_kernel, [(pieces.shape[1:], f32), ((8, 128), f32)], pieces)


def add_pair_kernel(one_ref, two_ref, out_ref):
    out_ref[...] = jnp.broadcast_to(one_ref[...] + two_ref[...], out_ref.shape)


def add_pair(one, two):
    return local_call(add_pair_kernel, [((8, 8, 128), f32)], one, two)[0]


def late_kernel(squares_ref, shard_ref, out_ref):
    out_ref[:, :, :512] = jnp.broadcast_to(shard_ref[...].astype(bf16), (32, 16, 512))
    rest = jnp.sum(squares_ref[...], axis=0)
    lane = lax.broadcasted_iota(jnp.int32, (8, 128), 1)
    beside = jnp.zeros((8, 128), f32)
    for k in range(3):
        term = rest.astype(bf16).astype(f32)
        rest = rest - term
        beside = jnp.where(lane == k, term, beside)
    beside = jnp.concatenate([beside, beside], axis=0).astype(bf16)
    out_ref[:, :, 512:] = jnp.broadcast_to(beside, (32, 16, 128))


def late_rows(squares, shard):
    return local_call(late_kernel, [((32, 16, 640), bf16)], squares, shard)[0]


def update_kernel(gathered_ref, state_ref, shard_ref, first_ref, second_ref, weight_out, first_out, second_out):
    terms = jnp.sum(gathered_ref[:, :, 512:].astype(f32), axis=0)
    total_square = jnp.sum(terms[:1], axis=1, keepdims=True)
    clip_limit = math.sqrt(KV * D)
    clip_factor = jnp.minimum(1.0, clip_limit / (jnp.sqrt(total_square) + 1e-06))

    def moments(gradient, first, second):
        clipped = gradient * clip_factor
        return (
            beta_one * first + (1.0 - beta_one) * clipped,
            beta_two * second + (1.0 - beta_two) * clipped * clipped,
        )

    new_first, new_second = moments(shard_ref[...], first_ref[...], second_ref[...])
    first_out[...] = new_first
    second_out[...] = new_second
    for r in range(32):
        rows = slice(r * 16, (r + 1) * 16)
        state = state_ref[rows].astype(f32)
        new_first, new_second = moments(gathered_ref[r, :, :512].astype(f32), state[:, 512:1024], state[:, 1024:])
        weight_out[rows] = (
            state[:, :512] * (1.0 - learn_rate * decay_rate)
            - learn_rate * new_first / (jnp.sqrt(new_second) + eps_adam)
        ).astype(bf16)


def update(gathered, state, shard, first, second):
    outs = [((KV, 512), bf16), (first.shape, f32), (second.shape, f32)]
    return local_call(update_kernel, outs, gathered, state, shard, first, second)


def body(norm_input, key_grad, positions, norm_gain, key_weight, first_moment, second_moment):
    gain = norm_gain[None, :]
    core = lax.axis_index("c")
    cosine, sine = rotation(positions)
    send, keys, scale = prepare(norm_input, key_grad, cosine, sine, gain)

    state = jnp.concatenate([key_weight, first_moment.astype(bf16), second_moment.astype(bf16)], axis=1)
    state = exchange(copies_for(state, N_GROUP), GROUP).reshape(N_GROUP * 16, 3 * 512)
    send, state = lax.optimization_barrier((send, state))

    half = lax.dynamic_slice_in_dim(state, core * 256, 256, 1)
    own = lax.all_gather(half, ("yh", "yl", "z"), axis=0, tiled=True).reshape(2, 4, 8, 128, 256)

    received = exchange(send, GROUP)
    state, received = lax.optimization_barrier((state, received))
    state = lax.all_gather(state, "yl", axis=0, tiled=True)

    partial = product(received).reshape(N_PLANE, 16, 512)
    pieces = exchange(partial, PLANE)
    piece, square = add_pieces(pieces)
    own, _ = lax.optimization_barrier((own, piece))
    other = lax.ppermute(own, "c", [(0, 1), (1, 0)])

    swap = [(i * 8 + k, k * 8 + i) for i in range(8) for k in range(8)]
    grad_shard = lax.ppermute(piece, ("x", "c", "z"), swap)
    square = add_pair(square, lax.ppermute(square, "yh", [(0, 1), (1, 0)]))
    late = late_rows(exchange(square, "z"), grad_shard)
    late, other, own = lax.optimization_barrier((late, other, own))
    gathered = exchange(late, DP)
    input_grad = backward(core.astype(jnp.int32).reshape(1), keys, own, other, norm_input, scale, gain)
    state, input_grad = lax.optimization_barrier((state, input_grad))
    new_weight, new_first, new_second = update(gathered, state, grad_shard, first_moment, second_moment)
    return (input_grad, new_weight, new_first, new_second)


def solution(mesh):
    split = Mesh(mesh.devices.reshape(4, 4, 2, 8, 2), ("yl", "x", "c", "z", "yh"))
    placed = (
        P(DP_TENSOR, None),
        P(DP_TENSOR, None),
        P(DP_TENSOR),
        P(),
        P(DP, TENSOR),
        P(DP, TENSOR),
        P(DP, TENSOR),
    )
    return jax.shard_map(
        body,
        mesh=split,
        in_specs=placed,
        out_specs=(P(DP_TENSOR, None), P(None, TENSOR), P(DP, TENSOR), P(DP, TENSOR)),
        check_vma=False,
    )
```

```python
import math

import jax
import jax.numpy as jnp
from jax import lax
from jax.experimental import pallas as pl
from jax.experimental.pallas import tpu as pltpu
from jax.sharding import Mesh
from jax.sharding import PartitionSpec as P

D = 8192
KV_HEADS = 4
HEAD = 128
KV = KV_HEADS * HEAD
DP = ("yl", "x", "c")
TENSOR = ("z", "yh")
DP_TENSOR = DP + TENSOR
GROUP = ("x", "c")
PLANE = ("yl", "z", "yh")
N_GROUP = 8
N_PLANE = 64
WIDE = D // N_GROUP
COLS = WIDE + KV

eps_norm = 1e-05
beta_one = 0.9
beta_two = 0.95
learn_rate = 0.0003
decay_rate = 0.1
eps_adam = 1e-08

bf16 = jnp.bfloat16
f32 = jnp.float32


def exchange(x, axes):
    return lax.all_to_all(x, axes, split_axis=0, concat_axis=0, tiled=True)


def copies_for(x, count):
    return jnp.broadcast_to(x, (count, *x.shape))


def rotation(positions):
    half_width = HEAD // 2
    frequency = 500000.0 ** (-(2.0 * jnp.arange(half_width, dtype=f32)) / HEAD)
    angles = positions.astype(f32)[:, None] * frequency[None, :]
    cosine = jnp.cos(angles)
    sine = jnp.sin(angles)
    return cosine, sine


def prepare_kernel(x_ref, key_ref, cos_ref, sin_ref, gain_ref, send_ref, key_out_ref, scale_ref, gain_out_ref):
    x = x_ref[...].astype(f32)
    scale = lax.rsqrt(jnp.sum(x * x, axis=1, keepdims=True) / D + eps_norm)
    scale_ref[...] = jnp.broadcast_to(scale, scale_ref.shape)
    gain = gain_ref[...].astype(f32)
    gain_out_ref[...] = gain
    for k in range(D // HEAD):
        j, at = divmod(k * HEAD, WIDE)
        part = x_ref[:, k * HEAD : (k + 1) * HEAD].astype(f32)
        send_ref[j, :, at : at + HEAD] = (part * scale * gain[k : k + 1]).astype(bf16)
    cosine = jnp.concatenate([cos_ref[...], cos_ref[...]], axis=1)
    sine = jnp.concatenate([sin_ref[...], -sin_ref[...]], axis=1)
    for h in range(KV_HEADS):
        part = key_ref[:, h * HEAD : (h + 1) * HEAD].astype(f32)
        turned = part * cosine + pltpu.roll(part, HEAD // 2, 1) * sine
        turned = turned.astype(bf16)
        key_out_ref[:, h * HEAD : (h + 1) * HEAD] = turned
        for j in range(N_GROUP):
            send_ref[j, :, WIDE + h * HEAD : WIDE + (h + 1) * HEAD] = turned


def prepare(x, key_grad, cosine, sine, gain):
    tokens = x.shape[0]
    tile = 32
    return pl.pallas_call(
        prepare_kernel,
        grid=(tokens // tile,),
        in_specs=[
            pl.BlockSpec((tile, D), lambda i: (i, 0)),
            pl.BlockSpec((tile, KV), lambda i: (i, 0)),
            pl.BlockSpec((tile, HEAD // 2), lambda i: (i, 0)),
            pl.BlockSpec((tile, HEAD // 2), lambda i: (i, 0)),
            pl.BlockSpec(gain.shape, lambda i: (0, 0)),
        ],
        out_specs=[
            pl.BlockSpec((N_GROUP, tile, COLS), lambda i: (0, i, 0)),
            pl.BlockSpec((tile, KV), lambda i: (i, 0)),
            pl.BlockSpec((tile, HEAD), lambda i: (i, 0)),
            pl.BlockSpec(gain.shape, lambda i: (0, 0)),
        ],
        out_shape=[
            jax.ShapeDtypeStruct((N_GROUP, tokens, COLS), bf16),
            jax.ShapeDtypeStruct((tokens, KV), bf16),
            jax.ShapeDtypeStruct((tokens, HEAD), f32),
            jax.ShapeDtypeStruct(gain.shape, f32),
        ],
        compiler_params=pltpu.CompilerParams(vmem_limit_bytes=56 * 1024 * 1024),
        cost_estimate=pl.CostEstimate(flops=8 * tokens * D, bytes_accessed=6 * 1024 * 1024, transcendentals=0),
    )(x, key_grad, cosine, sine, gain)


def product_kernel(key_ref, normed_ref, out_ref):
    tokens = key_ref.shape[0] * key_ref.shape[1]
    keys = key_ref[...].reshape(tokens, KV)
    normed = normed_ref[...].reshape(tokens, normed_ref.shape[2])
    total = lax.dot_general(keys, normed, (((0,), (0,)), ((), ())), preferred_element_type=f32)
    out_ref[...] = total.astype(bf16).reshape(out_ref.shape)


def product(received):
    count, tokens, _ = received.shape
    half = WIDE // 2
    return pl.pallas_call(
        product_kernel,
        grid=(2,),
        in_specs=[
            pl.BlockSpec((count, tokens, KV), lambda h: (0, 0, WIDE // KV)),
            pl.BlockSpec((count, tokens, half), lambda h: (0, 0, h)),
        ],
        out_specs=pl.BlockSpec((32, 1, 16, half), lambda h: (0, h, 0, 0)),
        out_shape=jax.ShapeDtypeStruct((32, 2, 16, half), bf16),
        compiler_params=pltpu.CompilerParams(vmem_limit_bytes=32 * 1024 * 1024),
        cost_estimate=pl.CostEstimate(
            flops=2 * count * tokens * KV * WIDE, bytes_accessed=4 * 1024 * 1024, transcendentals=0
        ),
    )(received, received)


def backward_kernel(
    core_ref, key_ref, own_ref, other_ref, x_ref, scale_ref, gain_ref, out_ref, held, cross
):
    step = pl.program_id(0)
    core = core_ref[0]
    half = own_ref.shape[4]
    width = 2 * half
    first = step * own_ref.shape[2] * 2

    @pl.when(step == 0)
    def _():
        cross[...] = jnp.zeros_like(cross)

    total = jnp.zeros(cross.shape, f32)
    for z in range(own_ref.shape[2]):
        for yh in range(2):
            block = first + z * 2 + yh
            for side, ref in ((core, own_ref), (1 - core, other_ref)):
                up = jnp.dot(key_ref[...], ref[yh, :, z].reshape(KV, half), preferred_element_type=f32)
                for k in range(half // HEAD):
                    group = block * (width // HEAD) + side * (half // HEAD) + k
                    columns = pl.ds(pl.multiple_of(group * HEAD, HEAD), HEAD)
                    inside = pl.ds(pl.multiple_of(side * half + k * HEAD, HEAD), HEAD)
                    weighted = up[:, k * HEAD : (k + 1) * HEAD] * gain_ref[pl.ds(group, 1), :]
                    held[block, :, inside] = weighted
                    total += weighted * x_ref[:, columns].astype(f32)
    cross[...] += total

    @pl.when(step == pl.num_programs(0) - 1)
    def _():
        scale = scale_ref[:, :1]
        inner = scale * scale * (jnp.sum(cross[...], axis=1, keepdims=True) / D)
        for t in range(D // width):
            part = slice(t * width, (t + 1) * width)
            x = x_ref[:, part].astype(f32)
            out_ref[:, part] = (scale * (held[t] - x * inner)).astype(bf16)


def backward(core, keys, own, other, x, scale, gain):
    tokens = x.shape[0]
    width = 512
    deep = 2
    steps = 8 // deep
    weights = pl.BlockSpec((2, 4, deep, 128, width // 2), lambda t, core: (0, 0, t, 0, 0))
    whole = lambda a: pl.BlockSpec(a.shape, lambda t, core: (0, 0))
    return pl.pallas_call(
        backward_kernel,
        grid_spec=pltpu.PrefetchScalarGridSpec(
            num_scalar_prefetch=1,
            grid=(steps,),
            in_specs=[whole(keys), weights, weights, whole(x), whole(scale), whole(gain)],
            out_specs=pl.BlockSpec((tokens, D), lambda t, core: (0, 0)),
            scratch_shapes=[pltpu.VMEM((D // width, tokens, width), f32), pltpu.VMEM((tokens, HEAD), f32)],
        ),
        out_shape=jax.ShapeDtypeStruct((tokens, D), bf16),
        compiler_params=pltpu.CompilerParams(vmem_limit_bytes=56 * 1024 * 1024),
        cost_estimate=pl.CostEstimate(
            flops=2 * tokens * KV * D, bytes_accessed=12 * 1024 * 1024, transcendentals=0
        ),
    )(core, keys, own, other, x, scale, gain)


def local_call(kernel, outs, *args):
    return pl.pallas_call(
        kernel,
        out_shape=[jax.ShapeDtypeStruct(shape, kind) for shape, kind in outs],
        compiler_params=pltpu.CompilerParams(vmem_limit_bytes=32 * 1024 * 1024),
    )(*args)


def add_pieces_kernel(pieces_ref, piece_ref, square_ref):
    piece = jnp.sum(pieces_ref[...].astype(f32), axis=0)
    piece_ref[...] = piece
    square = jnp.sum(jnp.sum(piece * piece, axis=0, keepdims=True), axis=1, keepdims=True)
    square_ref[...] = jnp.broadcast_to(square, square_ref.shape)


def add_pieces(pieces):
    return local_call(add_pieces_kernel, [(pieces.shape[1:], f32), ((8, 128), f32)], pieces)


def add_pair_kernel(one_ref, two_ref, out_ref):
    out_ref[...] = jnp.broadcast_to(one_ref[...] + two_ref[...], out_ref.shape)


def add_pair(one, two):
    return local_call(add_pair_kernel, [((8, 8, 128), f32)], one, two)[0]


def late_kernel(squares_ref, shard_ref, out_ref):
    out_ref[:, :, :512] = jnp.broadcast_to(shard_ref[...].astype(bf16), (32, 16, 512))
    rest = jnp.sum(squares_ref[...], axis=0)
    lane = lax.broadcasted_iota(jnp.int32, (8, 128), 1)
    beside = jnp.zeros((8, 128), f32)
    for k in range(3):
        term = rest.astype(bf16).astype(f32)
        rest = rest - term
        beside = jnp.where(lane == k, term, beside)
    beside = jnp.concatenate([beside, beside], axis=0).astype(bf16)
    out_ref[:, :, 512:] = jnp.broadcast_to(beside, (32, 16, 128))


def late_rows(squares, shard):
    return local_call(late_kernel, [((32, 16, 640), bf16)], squares, shard)[0]


def update_kernel(
    place_ref, gathered_ref, own_ref, other_ref, m0_ref, m1_ref, m2_ref, m3_ref, shard_ref, first_ref, second_ref,
    weight_out, first_out, second_out,
):
    terms = jnp.sum(gathered_ref[:, :, 512:].astype(f32), axis=0)
    total_square = jnp.sum(terms[:1], axis=1, keepdims=True)
    clip_limit = math.sqrt(KV * D)
    clip_factor = jnp.minimum(1.0, clip_limit / (jnp.sqrt(total_square) + 1e-06))

    def moments(gradient, first, second):
        clipped = gradient * clip_factor
        return (
            beta_one * first + (1.0 - beta_one) * clipped,
            beta_two * second + (1.0 - beta_two) * clipped * clipped,
        )

    new_first, new_second = moments(shard_ref[...], first_ref[...], second_ref[...])
    first_out[...] = new_first
    second_out[...] = new_second
    core, yl = place_ref[0], place_ref[1]
    half = own_ref.shape[1]
    for k, ref in enumerate((m0_ref, m1_ref, m2_ref, m3_ref)):
        block = yl ^ k
        for r in range(8):
            part = slice(r * 16, (r + 1) * 16)
            rows = pl.ds(pl.multiple_of(block * 128 + r * 16, 16), 16)
            gradient = gathered_ref[block * 8 + r, :, :512].astype(f32)
            new_first, new_second = moments(gradient, ref[part, :512].astype(f32), ref[part, 512:].astype(f32))
            step = learn_rate * new_first / (jnp.sqrt(new_second) + eps_adam)
            own = own_ref[rows, :].astype(f32)
            other = other_ref[rows, :].astype(f32)
            for side in range(2):
                inside = slice(side * half, (side + 1) * half)
                weight = jnp.where(core == side, own, other)
                weight_out[rows, inside] = (weight * (1.0 - learn_rate * decay_rate) - step[:, inside]).astype(bf16)


def update(place, *args):
    shard = args[-1]
    return pl.pallas_call(
        update_kernel,
        in_specs=[pl.BlockSpec(memory_space=pltpu.SMEM)] + [pl.BlockSpec(memory_space=pltpu.VMEM)] * len(args),
        out_specs=[pl.BlockSpec(memory_space=pltpu.VMEM)] * 3,
        out_shape=[jax.ShapeDtypeStruct(s, k) for s, k in (((KV, 512), bf16), (shard.shape, f32), (shard.shape, f32))],
        compiler_params=pltpu.CompilerParams(vmem_limit_bytes=32 * 1024 * 1024),
    )(place, *args)


def state_kernel(weight_ref, first_ref, second_ref, out_ref):
    out_ref[:, :, :512] = jnp.broadcast_to(weight_ref[...], (N_GROUP, 16, 512))
    out_ref[:, :, 512:1024] = jnp.broadcast_to(first_ref[...].astype(bf16), (N_GROUP, 16, 512))
    out_ref[:, :, 1024:] = jnp.broadcast_to(second_ref[...].astype(bf16), (N_GROUP, 16, 512))


def body(norm_input, key_grad, positions, norm_gain, key_weight, first_moment, second_moment):
    core = lax.axis_index("c")
    state = local_call(state_kernel, [((N_GROUP, 16, 1536), bf16)], key_weight, first_moment, second_moment)[0]
    state = exchange(state, GROUP).reshape(N_GROUP * 16, 1536)
    cosine, sine = rotation(positions)
    send, keys, scale, gain = prepare(norm_input, key_grad, cosine, sine, norm_gain.reshape(D // HEAD, HEAD))
    send, state = lax.optimization_barrier((send, state))

    half = lax.dynamic_slice_in_dim(state, core * 256, 256, 1)
    own = lax.all_gather(half, ("yh", "yl", "z"), axis=0, tiled=True).reshape(2, 4, 8, 128, 256)

    received = exchange(send, GROUP)
    moments = [state[:, 512:]]
    moments += [lax.ppermute(moments[0], "yl", [(i, i ^ k) for i in range(4)]) for k in (1, 2, 3)]
    received, *moments = lax.optimization_barrier((received, *moments))
    partial = product(received).reshape(N_PLANE, 16, 512)
    pieces = exchange(partial, PLANE)
    piece, square = add_pieces(pieces)

    swap = [(i * 8 + k, k * 8 + i) for i in range(8) for k in range(8)]
    grad_shard = lax.ppermute(piece, ("x", "c", "z"), swap)
    square = add_pair(square, lax.ppermute(square, "yh", [(0, 1), (1, 0)]))
    own, _ = lax.optimization_barrier((own, square))
    other = lax.ppermute(own, "c", [(0, 1), (1, 0)])
    late = late_rows(exchange(square, "z"), grad_shard)
    late, own, other = lax.optimization_barrier((late, own, other))
    gathered = exchange(late, DP)
    input_grad = backward(core.astype(jnp.int32).reshape(1), keys, own, other, norm_input, scale, gain)
    own, other, input_grad = lax.optimization_barrier((own, other, input_grad))
    z, yh = lax.axis_index("z"), lax.axis_index("yh")
    weights = [lax.dynamic_slice(w, (yh, 0, z, 0, 0), (1, 4, 1, 128, 256)).reshape(KV, 256) for w in (own, other)]
    place = jnp.stack([core, lax.axis_index("yl")]).astype(jnp.int32)
    new_weight, new_first, new_second = update(
        place, gathered, *weights, *moments, grad_shard, first_moment, second_moment
    )
    return (input_grad, new_weight, new_first, new_second)


def solution(mesh):
    split = Mesh(mesh.devices.reshape(4, 4, 2, 8, 2), ("yl", "x", "c", "z", "yh"))
    placed = (
        P(DP_TENSOR, None),
        P(DP_TENSOR, None),
        P(DP_TENSOR),
        P(),
        P(DP, TENSOR),
        P(DP, TENSOR),
        P(DP, TENSOR),
    )
    return jax.shard_map(
        body,
        mesh=split,
        in_specs=placed,
        out_specs=(P(DP_TENSOR, None), P(None, TENSOR), P(DP, TENSOR), P(DP, TENSOR)),
        check_vma=False,
    )
```

```python
import math

import jax
import jax.numpy as jnp
from jax import lax
from jax.experimental import pallas as pl
from jax.experimental.pallas import tpu as pltpu
from jax.sharding import Mesh
from jax.sharding import PartitionSpec as P

D = 8192
KV_HEADS = 4
HEAD = 128
KV = KV_HEADS * HEAD
DP = ("yl", "x", "c")
TENSOR = ("z", "yh")
DP_TENSOR = DP + TENSOR
GROUP = ("x", "c")
PLANE = ("yl", "z", "yh")
N_GROUP = 8
N_PLANE = 64
WIDE = D // N_GROUP
COLS = WIDE + KV

eps_norm = 1e-05
beta_one = 0.9
beta_two = 0.95
learn_rate = 0.0003
decay_rate = 0.1
eps_adam = 1e-08

bf16 = jnp.bfloat16
f32 = jnp.float32


def exchange(x, axes):
    return lax.all_to_all(x, axes, split_axis=0, concat_axis=0, tiled=True)


def copies_for(x, count):
    return jnp.broadcast_to(x, (count, *x.shape))


def rotation(positions):
    half_width = HEAD // 2
    frequency = 500000.0 ** (-(2.0 * jnp.arange(half_width, dtype=f32)) / HEAD)
    angles = positions.astype(f32)[:, None] * frequency[None, :]
    cosine = jnp.cos(angles)
    sine = jnp.sin(angles)
    return cosine, sine


def prepare_kernel(x_ref, key_ref, cos_ref, sin_ref, gain_ref, send_ref, key_out_ref, scale_ref, gain_out_ref):
    x = x_ref[...].astype(f32)
    scale = lax.rsqrt(jnp.sum(x * x, axis=1, keepdims=True) / D + eps_norm)
    scale_ref[...] = jnp.broadcast_to(scale, scale_ref.shape)
    gain = gain_ref[...].astype(f32)
    gain_out_ref[...] = gain
    for k in range(D // HEAD):
        j, at = divmod(k * HEAD, WIDE)
        part = x_ref[:, k * HEAD : (k + 1) * HEAD].astype(f32)
        send_ref[j, :, at : at + HEAD] = (part * scale * gain[k : k + 1]).astype(bf16)
    cosine = jnp.concatenate([cos_ref[...], cos_ref[...]], axis=1)
    sine = jnp.concatenate([sin_ref[...], -sin_ref[...]], axis=1)
    for h in range(KV_HEADS):
        part = key_ref[:, h * HEAD : (h + 1) * HEAD].astype(f32)
        turned = part * cosine + pltpu.roll(part, HEAD // 2, 1) * sine
        turned = turned.astype(bf16)
        key_out_ref[:, h * HEAD : (h + 1) * HEAD] = turned
        for j in range(N_GROUP):
            send_ref[j, :, WIDE + h * HEAD : WIDE + (h + 1) * HEAD] = turned


def prepare(x, key_grad, cosine, sine, gain):
    tokens = x.shape[0]
    tile = 32
    return pl.pallas_call(
        prepare_kernel,
        grid=(tokens // tile,),
        in_specs=[
            pl.BlockSpec((tile, D), lambda i: (i, 0)),
            pl.BlockSpec((tile, KV), lambda i: (i, 0)),
            pl.BlockSpec((tile, HEAD // 2), lambda i: (i, 0)),
            pl.BlockSpec((tile, HEAD // 2), lambda i: (i, 0)),
            pl.BlockSpec(gain.shape, lambda i: (0, 0)),
        ],
        out_specs=[
            pl.BlockSpec((N_GROUP, tile, COLS), lambda i: (0, i, 0)),
            pl.BlockSpec((tile, KV), lambda i: (i, 0)),
            pl.BlockSpec((tile, HEAD), lambda i: (i, 0)),
            pl.BlockSpec(gain.shape, lambda i: (0, 0)),
        ],
        out_shape=[
            jax.ShapeDtypeStruct((N_GROUP, tokens, COLS), bf16),
            jax.ShapeDtypeStruct((tokens, KV), bf16),
            jax.ShapeDtypeStruct((tokens, HEAD), f32),
            jax.ShapeDtypeStruct(gain.shape, f32),
        ],
        compiler_params=pltpu.CompilerParams(vmem_limit_bytes=56 * 1024 * 1024),
        cost_estimate=pl.CostEstimate(flops=8 * tokens * D, bytes_accessed=6 * 1024 * 1024, transcendentals=0),
    )(x, key_grad, cosine, sine, gain)


def product_kernel(key_ref, normed_ref, out_ref):
    tokens = key_ref.shape[0] * key_ref.shape[1]
    keys = key_ref[...].reshape(tokens, KV)
    normed = normed_ref[...].reshape(tokens, normed_ref.shape[2])
    total = lax.dot_general(keys, normed, (((0,), (0,)), ((), ())), preferred_element_type=f32)
    out_ref[...] = total.astype(bf16).reshape(out_ref.shape)


def product(received):
    count, tokens, _ = received.shape
    half = WIDE // 2
    return pl.pallas_call(
        product_kernel,
        grid=(2,),
        in_specs=[
            pl.BlockSpec((count, tokens, KV), lambda h: (0, 0, WIDE // KV)),
            pl.BlockSpec((count, tokens, half), lambda h: (0, 0, h)),
        ],
        out_specs=pl.BlockSpec((32, 1, 16, half), lambda h: (0, h, 0, 0)),
        out_shape=jax.ShapeDtypeStruct((32, 2, 16, half), bf16),
        compiler_params=pltpu.CompilerParams(vmem_limit_bytes=32 * 1024 * 1024),
        cost_estimate=pl.CostEstimate(
            flops=2 * count * tokens * KV * WIDE, bytes_accessed=4 * 1024 * 1024, transcendentals=0
        ),
    )(received, received)


def backward_kernel(place_ref, key_ref, *refs):
    own, other = refs[:4], refs[4:8]
    x_ref, scale_ref, gain_ref, out_ref, held, cross, sorted_keys = refs[8:]
    step = pl.program_id(0)
    core, yl, x, z, yh = (place_ref[i] for i in range(5))
    deep, half = own[0].shape[0], own[0].shape[4]
    width = 2 * half

    @pl.when(step == 0)
    def _():
        cross[...] = jnp.zeros_like(cross)
        row = lax.broadcasted_iota(jnp.int32, (KV, KV), 0)
        at = lax.broadcasted_iota(jnp.int32, (KV, KV), 1)
        source = ((((at >> 5) & 3) ^ yl) * 4 + ((at >> 7) ^ x)) * 32 + (at & 31)
        order = jnp.where(row == source, 1.0, 0.0).astype(bf16)
        sorted_keys[...] = jnp.dot(key_ref[...], order, preferred_element_type=f32).astype(bf16)

    total = jnp.zeros(cross.shape, f32)
    for kz in range(deep):
        for kyh in range(2):
            block = (z ^ (step * deep + kz)) * 2 + (yh ^ kyh)
            for side, pieces in ((core, own), (1 - core, other)):
                weight = jnp.concatenate([p[kz, kyh].reshape(KV // 4, half) for p in pieces], axis=0)
                up = jnp.dot(sorted_keys[...], weight, preferred_element_type=f32)
                for k in range(half // HEAD):
                    group = block * (width // HEAD) + side * (half // HEAD) + k
                    columns = pl.ds(pl.multiple_of(group * HEAD, HEAD), HEAD)
                    inside = pl.ds(pl.multiple_of(side * half + k * HEAD, HEAD), HEAD)
                    weighted = up[:, k * HEAD : (k + 1) * HEAD] * gain_ref[pl.ds(group, 1), :]
                    held[block, :, inside] = weighted
                    total += weighted * x_ref[:, columns].astype(f32)
    cross[...] += total

    @pl.when(step == pl.num_programs(0) - 1)
    def _():
        scale = scale_ref[:, :1]
        inner = scale * scale * (jnp.sum(cross[...], axis=1, keepdims=True) / D)
        for t in range(D // width):
            part = slice(t * width, (t + 1) * width)
            x_part = x_ref[:, part].astype(f32)
            out_ref[:, part] = (scale * (held[t] - x_part * inner)).astype(bf16)


def backward(place, keys, own, other, x, scale, gain):
    tokens = x.shape[0]
    width = 512
    deep = 2
    steps = 8 // deep
    weights = pl.BlockSpec((deep, *own[0].shape[1:]), lambda t, place: (t, 0, 0, 0, 0))
    whole = lambda a: pl.BlockSpec(a.shape, lambda t, place: (0, 0))
    return pl.pallas_call(
        backward_kernel,
        grid_spec=pltpu.PrefetchScalarGridSpec(
            num_scalar_prefetch=1,
            grid=(steps,),
            in_specs=[whole(keys)] + [weights] * 8 + [whole(x), whole(scale), whole(gain)],
            out_specs=pl.BlockSpec((tokens, D), lambda t, place: (0, 0)),
            scratch_shapes=[
                pltpu.VMEM((D // width, tokens, width), f32),
                pltpu.VMEM((tokens, HEAD), f32),
                pltpu.VMEM((tokens, KV), bf16),
            ],
        ),
        out_shape=jax.ShapeDtypeStruct((tokens, D), bf16),
        compiler_params=pltpu.CompilerParams(vmem_limit_bytes=56 * 1024 * 1024),
        cost_estimate=pl.CostEstimate(
            flops=2 * tokens * KV * D, bytes_accessed=12 * 1024 * 1024, transcendentals=0
        ),
    )(place, keys, *own, *other, x, scale, gain)


def local_call(kernel, outs, *args, vmem=32):
    return pl.pallas_call(
        kernel,
        out_shape=[jax.ShapeDtypeStruct(shape, kind) for shape, kind in outs],
        compiler_params=pltpu.CompilerParams(vmem_limit_bytes=vmem * 1024 * 1024),
    )(*args)


def stack_kernel(*refs):
    for k, ref in enumerate(refs[:-1]):
        refs[-1][k] = ref[...]


def from_others(x, axis):
    return [lax.ppermute(x, axis, [(i, i ^ k) for i in range(lax.axis_size(axis))]) for k in range(1, lax.axis_size(axis))]


def stacked(x, axis):
    parts = [x, *from_others(x, axis)]
    return local_call(stack_kernel, [((len(parts), *x.shape), x.dtype)], *parts)[0]


def add_pieces_kernel(pieces_ref, piece_ref, square_ref):
    piece = jnp.sum(pieces_ref[...].astype(f32), axis=0)
    piece_ref[...] = piece
    square = jnp.sum(jnp.sum(piece * piece, axis=0, keepdims=True), axis=1, keepdims=True)
    square_ref[...] = jnp.broadcast_to(square, square_ref.shape)


def add_pieces(pieces):
    return local_call(add_pieces_kernel, [(pieces.shape[1:], f32), ((8, 128), f32)], pieces)


def add_pair_kernel(one_ref, two_ref, out_ref):
    out_ref[...] = jnp.broadcast_to(one_ref[...] + two_ref[...], out_ref.shape)


def add_pair(one, two):
    return local_call(add_pair_kernel, [((8, 8, 128), f32)], one, two)[0]


def late_kernel(squares_ref, shard_ref, out_ref):
    out_ref[:, :, :512] = jnp.broadcast_to(shard_ref[...].astype(bf16), (32, 16, 512))
    rest = jnp.sum(squares_ref[...], axis=0)
    lane = lax.broadcasted_iota(jnp.int32, (8, 128), 1)
    beside = jnp.zeros((8, 128), f32)
    for k in range(3):
        term = rest.astype(bf16).astype(f32)
        rest = rest - term
        beside = jnp.where(lane == k, term, beside)
    beside = jnp.concatenate([beside, beside], axis=0).astype(bf16)
    out_ref[:, :, 512:] = jnp.broadcast_to(beside, (32, 16, 128))


def late_rows(squares, shard):
    return local_call(late_kernel, [((32, 16, 640), bf16)], squares, shard)[0]


def update_kernel(
    place_ref, gathered_ref, s0_ref, s1_ref, s2_ref, s3_ref, shard_ref, first_ref, second_ref,
    weight_out, first_out, second_out,
):
    terms = jnp.sum(gathered_ref[:, :, 512:].astype(f32), axis=0)
    total_square = jnp.sum(terms[:1], axis=1, keepdims=True)
    clip_limit = math.sqrt(KV * D)
    clip_factor = jnp.minimum(1.0, clip_limit / (jnp.sqrt(total_square) + 1e-06))

    def moments(gradient, first, second):
        clipped = gradient * clip_factor
        return (
            beta_one * first + (1.0 - beta_one) * clipped,
            beta_two * second + (1.0 - beta_two) * clipped * clipped,
        )

    new_first, new_second = moments(shard_ref[...], first_ref[...], second_ref[...])
    first_out[...] = new_first
    second_out[...] = new_second
    for k, ref in enumerate((s0_ref, s1_ref, s2_ref, s3_ref)):
        block = place_ref[1] ^ k
        for r in range(8):
            rows = pl.ds(pl.multiple_of(block * 128 + r * 16, 16), 16)
            gradient = gathered_ref[block * 8 + r, :, :512].astype(f32)
            state = ref[r * 16 : (r + 1) * 16, :].astype(f32)
            new_first, new_second = moments(gradient, state[:, 512:1024], state[:, 1024:])
            weight_out[rows, :] = (
                state[:, :512] * (1.0 - learn_rate * decay_rate)
                - learn_rate * new_first / (jnp.sqrt(new_second) + eps_adam)
            ).astype(bf16)


def update(place, *args):
    shard = args[-1]
    return pl.pallas_call(
        update_kernel,
        in_specs=[pl.BlockSpec(memory_space=pltpu.SMEM)] + [pl.BlockSpec(memory_space=pltpu.VMEM)] * len(args),
        out_specs=[pl.BlockSpec(memory_space=pltpu.VMEM)] * 3,
        out_shape=[jax.ShapeDtypeStruct(s, k) for s, k in (((KV, 512), bf16), (shard.shape, f32), (shard.shape, f32))],
        compiler_params=pltpu.CompilerParams(vmem_limit_bytes=32 * 1024 * 1024),
    )(place, *args)


def state_kernel(weight_ref, first_ref, second_ref, out_ref):
    out_ref[:, :, :512] = jnp.broadcast_to(weight_ref[...], (N_GROUP, 16, 512))
    out_ref[:, :, 512:1024] = jnp.broadcast_to(first_ref[...].astype(bf16), (N_GROUP, 16, 512))
    out_ref[:, :, 1024:] = jnp.broadcast_to(second_ref[...].astype(bf16), (N_GROUP, 16, 512))


def body(norm_input, key_grad, positions, norm_gain, key_weight, first_moment, second_moment):
    place = jnp.stack([lax.axis_index(name) for name in ("c", "yl", "x", "z", "yh")]).astype(jnp.int32)
    state = local_call(
        state_kernel, [((N_GROUP, 16, 1536), bf16)], key_weight, first_moment, second_moment, vmem=56
    )[0]
    state = exchange(state, GROUP)
    cosine, sine = rotation(positions)
    send, keys, scale, gain = prepare(norm_input, key_grad, cosine, sine, norm_gain.reshape(D // HEAD, HEAD))
    send, state = lax.optimization_barrier((send, state))

    received = exchange(send, GROUP)
    own = lax.dynamic_slice(state, (2 * place[2], 0, 256 * place[0]), (2, 16, 256)).reshape(32, 256)
    own = stacked(stacked(stacked(own, "yl"), "yh"), "z")
    state = state.reshape(N_GROUP * 16, 1536)
    states = [state, *from_others(state, "yl")]
    received, own, *states = lax.optimization_barrier((received, own, *states))

    partial = product(received).reshape(N_PLANE, 16, 512)
    own, partial = lax.optimization_barrier((own, partial))
    pieces = exchange(partial, PLANE)
    own = [own, *from_others(own, "x")]
    pieces, *own = lax.optimization_barrier((pieces, *own))
    piece, square = add_pieces(pieces)

    swap = [(i * 8 + k, k * 8 + i) for i in range(8) for k in range(8)]
    grad_shard = lax.ppermute(piece, ("x", "c", "z"), swap)
    square = add_pair(square, lax.ppermute(square, "yh", [(0, 1), (1, 0)]))
    *own, _ = lax.optimization_barrier((*own, square))
    other = [lax.ppermute(part, "c", [(0, 1), (1, 0)]) for part in own]
    late = late_rows(exchange(square, "z"), grad_shard)
    late, *halves = lax.optimization_barrier((late, *own, *other))
    gathered = exchange(late, DP)
    input_grad = backward(place, keys, halves[:4], halves[4:], norm_input, scale, gain)
    new_weight, new_first, new_second = update(
        place, gathered, *states, grad_shard, first_moment, second_moment
    )
    return (input_grad, new_weight, new_first, new_second)


def solution(mesh):
    split = Mesh(mesh.devices.reshape(4, 4, 2, 8, 2), ("yl", "x", "c", "z", "yh"))
    placed = (
        P(DP_TENSOR, None),
        P(DP_TENSOR, None),
        P(DP_TENSOR),
        P(),
        P(DP, TENSOR),
        P(DP, TENSOR),
        P(DP, TENSOR),
    )
    return jax.shard_map(
        body,
        mesh=split,
        in_specs=placed,
        out_specs=(P(DP_TENSOR, None), P(None, TENSOR), P(DP, TENSOR), P(DP, TENSOR)),
        check_vma=False,
    )
```

```python
import math

import jax
import jax.numpy as jnp
from jax import lax
from jax.experimental import pallas as pl
from jax.experimental.pallas import tpu as pltpu
from jax.sharding import Mesh
from jax.sharding import PartitionSpec as P

D = 8192
KV_HEADS = 4
HEAD = 128
KV = KV_HEADS * HEAD
DP = ("yl", "x", "c")
TENSOR = ("z", "yh")
DP_TENSOR = DP + TENSOR
GROUP = ("x", "c")
PLANE = ("yl", "z", "yh")
N_GROUP = 8
N_PLANE = 64
WIDE = D // N_GROUP
COLS = WIDE + KV

eps_norm = 1e-05
beta_one = 0.9
beta_two = 0.95
learn_rate = 0.0003
decay_rate = 0.1
eps_adam = 1e-08

bf16 = jnp.bfloat16
f32 = jnp.float32


def exchange(x, axes):
    return lax.all_to_all(x, axes, split_axis=0, concat_axis=0, tiled=True)


def rotation(positions):
    half_width = HEAD // 2
    frequency = 500000.0 ** (-(2.0 * jnp.arange(half_width, dtype=f32)) / HEAD)
    angles = positions.astype(f32)[:, None] * frequency[None, :]
    cosine = jnp.cos(angles)
    sine = jnp.sin(angles)
    return cosine, sine


def prepare_kernel(x_ref, key_ref, cos_ref, sin_ref, gain_ref, send_ref, key_out_ref, scale_ref, gain_out_ref):
    x = x_ref[...].astype(f32)
    scale = lax.rsqrt(jnp.sum(x * x, axis=1, keepdims=True) / D + eps_norm)
    scale_ref[...] = jnp.broadcast_to(scale, scale_ref.shape)
    gain = gain_ref[...].astype(f32)
    gain_out_ref[...] = gain
    for k in range(D // HEAD):
        j, at = divmod(k * HEAD, WIDE)
        part = x_ref[:, k * HEAD : (k + 1) * HEAD].astype(f32)
        send_ref[j, :, at : at + HEAD] = (part * scale * gain[k : k + 1]).astype(bf16)
    cosine = jnp.concatenate([cos_ref[...], cos_ref[...]], axis=1)
    sine = jnp.concatenate([sin_ref[...], -sin_ref[...]], axis=1)
    for h in range(KV_HEADS):
        part = key_ref[:, h * HEAD : (h + 1) * HEAD].astype(f32)
        turned = part * cosine + pltpu.roll(part, HEAD // 2, 1) * sine
        turned = turned.astype(bf16)
        key_out_ref[:, h * HEAD : (h + 1) * HEAD] = turned
        for j in range(N_GROUP):
            send_ref[j, :, WIDE + h * HEAD : WIDE + (h + 1) * HEAD] = turned


def prepare(x, key_grad, cosine, sine, gain):
    tokens = x.shape[0]
    tile = 32
    return pl.pallas_call(
        prepare_kernel,
        grid=(tokens // tile,),
        in_specs=[
            pl.BlockSpec((tile, D), lambda i: (i, 0)),
            pl.BlockSpec((tile, KV), lambda i: (i, 0)),
            pl.BlockSpec((tile, HEAD // 2), lambda i: (i, 0)),
            pl.BlockSpec((tile, HEAD // 2), lambda i: (i, 0)),
            pl.BlockSpec(gain.shape, lambda i: (0, 0)),
        ],
        out_specs=[
            pl.BlockSpec((N_GROUP, tile, COLS), lambda i: (0, i, 0)),
            pl.BlockSpec((tile, KV), lambda i: (i, 0)),
            pl.BlockSpec((tile, HEAD), lambda i: (i, 0)),
            pl.BlockSpec(gain.shape, lambda i: (0, 0)),
        ],
        out_shape=[
            jax.ShapeDtypeStruct((N_GROUP, tokens, COLS), bf16),
            jax.ShapeDtypeStruct((tokens, KV), bf16),
            jax.ShapeDtypeStruct((tokens, HEAD), f32),
            jax.ShapeDtypeStruct(gain.shape, f32),
        ],
        compiler_params=pltpu.CompilerParams(vmem_limit_bytes=56 * 1024 * 1024),
        cost_estimate=pl.CostEstimate(flops=8 * tokens * D, bytes_accessed=6 * 1024 * 1024, transcendentals=0),
    )(x, key_grad, cosine, sine, gain)


def product_kernel(key_ref, normed_ref, out_ref):
    tokens = key_ref.shape[0] * key_ref.shape[1]
    keys = key_ref[...].reshape(tokens, KV)
    normed = normed_ref[...].reshape(tokens, normed_ref.shape[2])
    total = lax.dot_general(keys, normed, (((0,), (0,)), ((), ())), preferred_element_type=f32)
    out_ref[...] = total.astype(bf16).reshape(out_ref.shape)


def product(received):
    count, tokens, _ = received.shape
    half = WIDE // 2
    return pl.pallas_call(
        product_kernel,
        grid=(2,),
        in_specs=[
            pl.BlockSpec((count, tokens, KV), lambda h: (0, 0, WIDE // KV)),
            pl.BlockSpec((count, tokens, half), lambda h: (0, 0, h)),
        ],
        out_specs=pl.BlockSpec((32, 1, 16, half), lambda h: (0, h, 0, 0)),
        out_shape=jax.ShapeDtypeStruct((32, 2, 16, half), bf16),
        compiler_params=pltpu.CompilerParams(vmem_limit_bytes=32 * 1024 * 1024),
        cost_estimate=pl.CostEstimate(
            flops=2 * count * tokens * KV * WIDE, bytes_accessed=4 * 1024 * 1024, transcendentals=0
        ),
    )(received, received)


def backward_kernel(key_ref, weight_ref, x_ref, scale_ref, gain_ref, out_ref, held, cross):
    step = pl.program_id(0)
    deep, width = weight_ref.shape[2], weight_ref.shape[4]

    @pl.when(step == 0)
    def _():
        cross[...] = jnp.zeros_like(cross)

    total = jnp.zeros(cross.shape, f32)
    for z in range(deep):
        for yh in range(2):
            block = (step * deep + z) * 2 + yh
            up = jnp.dot(key_ref[...], weight_ref[yh, :, z].reshape(KV, width), preferred_element_type=f32)
            for k in range(width // HEAD):
                group = block * (width // HEAD) + k
                columns = pl.ds(pl.multiple_of(group * HEAD, HEAD), HEAD)
                inside = slice(k * HEAD, (k + 1) * HEAD)
                weighted = up[:, inside] * gain_ref[pl.ds(group, 1), :]
                held[block, :, inside] = weighted
                total += weighted * x_ref[:, columns].astype(f32)
    cross[...] += total

    @pl.when(step == pl.num_programs(0) - 1)
    def _():
        scale = scale_ref[:, :1]
        inner = scale * scale * (jnp.sum(cross[...], axis=1, keepdims=True) / D)
        for t in range(D // width):
            part = slice(t * width, (t + 1) * width)
            x = x_ref[:, part].astype(f32)
            out_ref[:, part] = (scale * (held[t] - x * inner)).astype(bf16)


def backward(keys, weights, x, scale, gain):
    tokens = x.shape[0]
    width = 512
    deep = 2
    steps = 8 // deep
    whole = lambda a: pl.BlockSpec(a.shape, lambda t: (0, 0))
    return pl.pallas_call(
        backward_kernel,
        grid=(steps,),
        in_specs=[
            whole(keys),
            pl.BlockSpec((2, 4, deep, 128, width), lambda t: (0, 0, t, 0, 0)),
            whole(x),
            whole(scale),
            whole(gain),
        ],
        out_specs=pl.BlockSpec((tokens, D), lambda t: (0, 0)),
        scratch_shapes=[pltpu.VMEM((D // width, tokens, width), f32), pltpu.VMEM((tokens, HEAD), f32)],
        out_shape=jax.ShapeDtypeStruct((tokens, D), bf16),
        compiler_params=pltpu.CompilerParams(vmem_limit_bytes=56 * 1024 * 1024),
        cost_estimate=pl.CostEstimate(
            flops=2 * tokens * KV * D, bytes_accessed=12 * 1024 * 1024, transcendentals=0
        ),
    )(keys, weights, x, scale, gain)


def local_call(kernel, outs, *args, vmem=32):
    return pl.pallas_call(
        kernel,
        out_shape=[jax.ShapeDtypeStruct(shape, kind) for shape, kind in outs],
        compiler_params=pltpu.CompilerParams(vmem_limit_bytes=vmem * 1024 * 1024),
    )(*args)


def from_others(x, axis):
    count = lax.axis_size(axis)
    return [lax.ppermute(x, axis, [(i, i ^ k) for i in range(count)]) for k in range(1, count)]


def add_pieces_kernel(pieces_ref, piece_ref, square_ref):
    piece = jnp.sum(pieces_ref[...].astype(f32), axis=0)
    piece_ref[...] = piece
    square = jnp.sum(jnp.sum(piece * piece, axis=0, keepdims=True), axis=1, keepdims=True)
    square_ref[...] = jnp.broadcast_to(square, square_ref.shape)


def add_pieces(pieces):
    return local_call(add_pieces_kernel, [(pieces.shape[1:], f32), ((N_PLANE, 128), f32)], pieces)


def late_kernel(squares_ref, s0_ref, s1_ref, s2_ref, s3_ref, out_ref):
    for k, ref in enumerate((s0_ref, s1_ref, s2_ref, s3_ref)):
        rows = slice(k * 16, (k + 1) * 16)
        out_ref[:, rows, :512] = jnp.broadcast_to(ref[...].astype(bf16), (N_GROUP, 16, 512))
    rest = jnp.broadcast_to(jnp.sum(squares_ref[...], axis=0, keepdims=True), (64, 128))
    lane = lax.broadcasted_iota(jnp.int32, (64, 128), 1)
    beside = jnp.zeros((64, 128), f32)
    for k in range(3):
        term = rest.astype(bf16).astype(f32)
        rest = rest - term
        beside = jnp.where(lane == k, term, beside)
    out_ref[:, :, 512:] = jnp.broadcast_to(beside.astype(bf16), (N_GROUP, 64, 128))


def late_rows(squares, shards):
    return local_call(late_kernel, [((N_GROUP, 64, 640), bf16)], squares, *shards)[0]


def update_kernel(
    place_ref, gathered_ref, weight_ref, m0_ref, m1_ref, m2_ref, m3_ref, shard_ref, first_ref, second_ref,
    weight_out, first_out, second_out,
):
    terms = jnp.sum(gathered_ref[:, :16, 512:].astype(f32), axis=0)
    total_square = jnp.sum(terms[:1], axis=1, keepdims=True)
    clip_limit = math.sqrt(KV * D)
    clip_factor = jnp.minimum(1.0, clip_limit / (jnp.sqrt(total_square) + 1e-06))

    def moments(gradient, first, second):
        clipped = gradient * clip_factor
        return (
            beta_one * first + (1.0 - beta_one) * clipped,
            beta_two * second + (1.0 - beta_two) * clipped * clipped,
        )

    new_first, new_second = moments(shard_ref[...], first_ref[...], second_ref[...])
    first_out[...] = new_first
    second_out[...] = new_second
    for k, ref in enumerate((m0_ref, m1_ref, m2_ref, m3_ref)):
        block = place_ref[0] ^ k
        for r in range(8):
            part = slice(r * 16, (r + 1) * 16)
            rows = pl.ds(pl.multiple_of(block * 128 + r * 16, 16), 16)
            gradient = gathered_ref[r, k * 16 : (k + 1) * 16, :512].astype(f32)
            new_first, new_second = moments(gradient, ref[part, :512].astype(f32), ref[part, 512:].astype(f32))
            weight_out[rows, :] = (
                weight_ref[rows, :].astype(f32) * (1.0 - learn_rate * decay_rate)
                - learn_rate * new_first / (jnp.sqrt(new_second) + eps_adam)
            ).astype(bf16)


def update(place, *args):
    shard = args[-1]
    return pl.pallas_call(
        update_kernel,
        in_specs=[pl.BlockSpec(memory_space=pltpu.SMEM)] + [pl.BlockSpec(memory_space=pltpu.VMEM)] * len(args),
        out_specs=[pl.BlockSpec(memory_space=pltpu.VMEM)] * 3,
        out_shape=[jax.ShapeDtypeStruct(s, k) for s, k in (((KV, 512), bf16), (shard.shape, f32), (shard.shape, f32))],
        compiler_params=pltpu.CompilerParams(vmem_limit_bytes=32 * 1024 * 1024),
    )(place, *args)


def state_kernel(weight_ref, first_ref, second_ref, out_ref):
    out_ref[:, :, :512] = jnp.broadcast_to(weight_ref[...], (N_GROUP, 16, 512))
    out_ref[:, :, 512:1024] = jnp.broadcast_to(first_ref[...].astype(bf16), (N_GROUP, 16, 512))
    out_ref[:, :, 1024:] = jnp.broadcast_to(second_ref[...].astype(bf16), (N_GROUP, 16, 512))


def body(norm_input, key_grad, positions, norm_gain, key_weight, first_moment, second_moment):
    state = local_call(
        state_kernel, [((N_GROUP, 16, 1536), bf16)], key_weight, first_moment, second_moment, vmem=56
    )[0]
    state = exchange(state, GROUP).reshape(N_GROUP * 16, 1536)
    cosine, sine = rotation(positions)
    send, keys, scale, gain = prepare(norm_input, key_grad, cosine, sine, norm_gain.reshape(D // HEAD, HEAD))
    send, state = lax.optimization_barrier((send, state))

    weights = lax.all_gather(state[:, :512], ("yh", "yl", "z"), axis=0, tiled=True).reshape(2, 4, 8, 128, 512)

    received = exchange(send, GROUP)
    moments = state[:, 512:]
    moments = [moments, *from_others(moments, "yl")]
    received, *moments = lax.optimization_barrier((received, *moments))
    partial = product(received).reshape(N_PLANE, 16, 512)
    pieces = exchange(partial, PLANE)
    piece, square = add_pieces(pieces)

    swap = [(i * 8 + k, k * 8 + i) for i in range(8) for k in range(8)]
    grad_shard = lax.ppermute(piece, ("x", "c", "z"), swap)
    shards = [grad_shard, *from_others(grad_shard, "yl")]
    late = late_rows(exchange(square, PLANE), shards)
    late, weights = lax.optimization_barrier((late, weights))
    gathered = exchange(late, GROUP)
    input_grad = backward(keys, weights, norm_input, scale, gain)
    weights, input_grad = lax.optimization_barrier((weights, input_grad))
    at = (lax.axis_index("yh"), 0, lax.axis_index("z"), 0, 0)
    weight = lax.dynamic_slice(weights, at, (1, 4, 1, 128, 512)).reshape(KV, 512)
    place = lax.axis_index("yl").astype(jnp.int32).reshape(1)
    new_weight, new_first, new_second = update(
        place, gathered, weight, *moments, grad_shard, first_moment, second_moment
    )
    return (input_grad, new_weight, new_first, new_second)


def solution(mesh):
    split = Mesh(mesh.devices.reshape(4, 4, 2, 8, 2), ("yl", "x", "c", "z", "yh"))
    placed = (
        P(DP_TENSOR, None),
        P(DP_TENSOR, None),
        P(DP_TENSOR),
        P(),
        P(DP, TENSOR),
        P(DP, TENSOR),
        P(DP, TENSOR),
    )
    return jax.shard_map(
        body,
        mesh=split,
        in_specs=placed,
        out_specs=(P(DP_TENSOR, None), P(None, TENSOR), P(DP, TENSOR), P(DP, TENSOR)),
        check_vma=False,
    )
```

```python
import math

import jax
import jax.numpy as jnp
from jax import lax
from jax.experimental import pallas as pl
from jax.experimental.pallas import tpu as pltpu
from jax.sharding import Mesh
from jax.sharding import PartitionSpec as P

D = 8192
KV_HEADS = 4
HEAD = 128
KV = KV_HEADS * HEAD
DP = ("yl", "x", "c")
TENSOR = ("z", "yh")
DP_TENSOR = DP + TENSOR
GROUP = ("x", "c")
PLANE = ("yl", "z", "yh")
N_GROUP = 8
N_PLANE = 64
WIDE = D // N_GROUP
COLS = WIDE + KV

eps_norm = 1e-05
beta_one = 0.9
beta_two = 0.95
learn_rate = 0.0003
decay_rate = 0.1
eps_adam = 1e-08

bf16 = jnp.bfloat16
f32 = jnp.float32


def exchange(x, axes):
    return lax.all_to_all(x, axes, split_axis=0, concat_axis=0, tiled=True)


def rotation(positions):
    half_width = HEAD // 2
    frequency = 500000.0 ** (-(2.0 * jnp.arange(half_width, dtype=f32)) / HEAD)
    angles = positions.astype(f32)[:, None] * frequency[None, :]
    cosine = jnp.cos(angles)
    sine = jnp.sin(angles)
    return cosine, sine


def prepare_kernel(x_ref, key_ref, cos_ref, sin_ref, gain_ref, send_ref, key_out_ref, scale_ref, gain_out_ref):
    x = x_ref[...].astype(f32)
    scale = lax.rsqrt(jnp.sum(x * x, axis=1, keepdims=True) / D + eps_norm)
    scale_ref[...] = jnp.broadcast_to(scale, scale_ref.shape)
    gain = gain_ref[...].astype(f32)
    gain_out_ref[...] = gain
    for k in range(D // HEAD):
        j, at = divmod(k * HEAD, WIDE)
        part = x_ref[:, k * HEAD : (k + 1) * HEAD].astype(f32)
        send_ref[j, :, at : at + HEAD] = (part * scale * gain[k : k + 1]).astype(bf16)
    cosine = jnp.concatenate([cos_ref[...], cos_ref[...]], axis=1)
    sine = jnp.concatenate([sin_ref[...], -sin_ref[...]], axis=1)
    for h in range(KV_HEADS):
        part = key_ref[:, h * HEAD : (h + 1) * HEAD].astype(f32)
        turned = part * cosine + pltpu.roll(part, HEAD // 2, 1) * sine
        turned = turned.astype(bf16)
        key_out_ref[:, h * HEAD : (h + 1) * HEAD] = turned
        for j in range(N_GROUP):
            send_ref[j, :, WIDE + h * HEAD : WIDE + (h + 1) * HEAD] = turned


def prepare(x, key_grad, cosine, sine, gain):
    tokens = x.shape[0]
    tile = 32
    return pl.pallas_call(
        prepare_kernel,
        grid=(tokens // tile,),
        in_specs=[
            pl.BlockSpec((tile, D), lambda i: (i, 0)),
            pl.BlockSpec((tile, KV), lambda i: (i, 0)),
            pl.BlockSpec((tile, HEAD // 2), lambda i: (i, 0)),
            pl.BlockSpec((tile, HEAD // 2), lambda i: (i, 0)),
            pl.BlockSpec(gain.shape, lambda i: (0, 0)),
        ],
        out_specs=[
            pl.BlockSpec((N_GROUP, tile, COLS), lambda i: (0, i, 0)),
            pl.BlockSpec((tile, KV), lambda i: (i, 0)),
            pl.BlockSpec((tile, HEAD), lambda i: (i, 0)),
            pl.BlockSpec(gain.shape, lambda i: (0, 0)),
        ],
        out_shape=[
            jax.ShapeDtypeStruct((N_GROUP, tokens, COLS), bf16),
            jax.ShapeDtypeStruct((tokens, KV), bf16),
            jax.ShapeDtypeStruct((tokens, HEAD), f32),
            jax.ShapeDtypeStruct(gain.shape, f32),
        ],
        compiler_params=pltpu.CompilerParams(vmem_limit_bytes=56 * 1024 * 1024),
        cost_estimate=pl.CostEstimate(flops=8 * tokens * D, bytes_accessed=6 * 1024 * 1024, transcendentals=0),
    )(x, key_grad, cosine, sine, gain)


def product_kernel(key_ref, normed_ref, out_ref):
    tokens = key_ref.shape[0] * key_ref.shape[1]
    keys = key_ref[...].reshape(tokens, KV)
    normed = normed_ref[...].reshape(tokens, normed_ref.shape[2])
    total = lax.dot_general(keys, normed, (((0,), (0,)), ((), ())), preferred_element_type=f32)
    out_ref[...] = total.astype(bf16).reshape(out_ref.shape)


def product(received):
    count, tokens, _ = received.shape
    half = WIDE // 2
    return pl.pallas_call(
        product_kernel,
        grid=(2,),
        in_specs=[
            pl.BlockSpec((count, tokens, KV), lambda h: (0, 0, WIDE // KV)),
            pl.BlockSpec((count, tokens, half), lambda h: (0, 0, h)),
        ],
        out_specs=pl.BlockSpec((32, 1, 16, half), lambda h: (0, h, 0, 0)),
        out_shape=jax.ShapeDtypeStruct((32, 2, 16, half), bf16),
        compiler_params=pltpu.CompilerParams(vmem_limit_bytes=32 * 1024 * 1024),
        cost_estimate=pl.CostEstimate(
            flops=2 * count * tokens * KV * WIDE, bytes_accessed=4 * 1024 * 1024, transcendentals=0
        ),
    )(received, received)


def backward_kernel(key_ref, weight_ref, x_ref, scale_ref, gain_ref, out_ref, held, cross):
    step = pl.program_id(0)
    deep, width = weight_ref.shape[2], weight_ref.shape[4]

    @pl.when(step == 0)
    def _():
        cross[...] = jnp.zeros_like(cross)

    total = jnp.zeros(cross.shape, f32)
    for z in range(deep):
        for yh in range(2):
            block = (step * deep + z) * 2 + yh
            up = jnp.dot(key_ref[...], weight_ref[yh, :, z].reshape(KV, width), preferred_element_type=f32)
            for k in range(width // HEAD):
                group = block * (width // HEAD) + k
                columns = pl.ds(pl.multiple_of(group * HEAD, HEAD), HEAD)
                inside = slice(k * HEAD, (k + 1) * HEAD)
                weighted = up[:, inside] * gain_ref[pl.ds(group, 1), :]
                held[block, :, inside] = weighted
                total += weighted * x_ref[:, columns].astype(f32)
    cross[...] += total

    @pl.when(step == pl.num_programs(0) - 1)
    def _():
        scale = scale_ref[:, :1]
        inner = scale * scale * (jnp.sum(cross[...], axis=1, keepdims=True) / D)
        for t in range(D // width):
            part = slice(t * width, (t + 1) * width)
            x = x_ref[:, part].astype(f32)
            out_ref[:, part] = (scale * (held[t] - x * inner)).astype(bf16)


def backward(keys, weights, x, scale, gain):
    tokens = x.shape[0]
    width = 512
    deep = 2
    steps = 8 // deep
    whole = lambda a: pl.BlockSpec(a.shape, lambda t: (0, 0))
    return pl.pallas_call(
        backward_kernel,
        grid=(steps,),
        in_specs=[
            whole(keys),
            pl.BlockSpec((2, 4, deep, 128, width), lambda t: (0, 0, t, 0, 0)),
            whole(x),
            whole(scale),
            whole(gain),
        ],
        out_specs=pl.BlockSpec((tokens, D), lambda t: (0, 0)),
        scratch_shapes=[pltpu.VMEM((D // width, tokens, width), f32), pltpu.VMEM((tokens, HEAD), f32)],
        out_shape=jax.ShapeDtypeStruct((tokens, D), bf16),
        compiler_params=pltpu.CompilerParams(vmem_limit_bytes=56 * 1024 * 1024),
        cost_estimate=pl.CostEstimate(
            flops=2 * tokens * KV * D, bytes_accessed=12 * 1024 * 1024, transcendentals=0
        ),
    )(keys, weights, x, scale, gain)


def local_call(kernel, outs, *args, vmem=32):
    return pl.pallas_call(
        kernel,
        out_shape=[jax.ShapeDtypeStruct(shape, kind) for shape, kind in outs],
        compiler_params=pltpu.CompilerParams(vmem_limit_bytes=vmem * 1024 * 1024),
    )(*args)


def from_others(x, axis):
    count = lax.axis_size(axis)
    return [lax.ppermute(x, axis, [(i, i ^ k) for i in range(count)]) for k in range(1, count)]


def add_pieces_kernel(pieces_ref, piece_ref, square_ref):
    piece = jnp.sum(pieces_ref[...].astype(f32), axis=0)
    piece_ref[...] = piece
    square = jnp.sum(jnp.sum(piece * piece, axis=0, keepdims=True), axis=1, keepdims=True)
    square_ref[...] = jnp.broadcast_to(square, square_ref.shape)


def add_pieces(pieces):
    return local_call(add_pieces_kernel, [(pieces.shape[1:], f32), ((N_PLANE, 128), f32)], pieces)


def late_kernel(squares_ref, s0_ref, s1_ref, s2_ref, s3_ref, out_ref):
    for k, ref in enumerate((s0_ref, s1_ref, s2_ref, s3_ref)):
        rows = slice(k * 16, (k + 1) * 16)
        out_ref[:, rows, :512] = jnp.broadcast_to(ref[...].astype(bf16), (N_GROUP, 16, 512))
    rest = jnp.broadcast_to(jnp.sum(squares_ref[...], axis=0, keepdims=True), (64, 128))
    lane = lax.broadcasted_iota(jnp.int32, (64, 128), 1)
    beside = jnp.zeros((64, 128), f32)
    for k in range(3):
        term = rest.astype(bf16).astype(f32)
        rest = rest - term
        beside = jnp.where(lane == k, term, beside)
    out_ref[:, :, 512:] = jnp.broadcast_to(beside.astype(bf16), (N_GROUP, 64, 128))


def late_rows(squares, shards):
    return local_call(late_kernel, [((N_GROUP, 64, 640), bf16)], squares, *shards)[0]


def update_kernel(
    place_ref, gathered_ref, weight_ref, m0_ref, m1_ref, m2_ref, m3_ref, shard_ref, first_ref, second_ref,
    weight_out, first_out, second_out,
):
    terms = jnp.sum(gathered_ref[:, :16, 512:].astype(f32), axis=0)
    total_square = jnp.sum(terms[:1], axis=1, keepdims=True)
    clip_limit = math.sqrt(KV * D)
    clip_factor = jnp.minimum(1.0, clip_limit / (jnp.sqrt(total_square) + 1e-06))

    def moments(gradient, first, second):
        clipped = gradient * clip_factor
        return (
            beta_one * first + (1.0 - beta_one) * clipped,
            beta_two * second + (1.0 - beta_two) * clipped * clipped,
        )

    new_first, new_second = moments(shard_ref[...], first_ref[...], second_ref[...])
    first_out[...] = new_first
    second_out[...] = new_second
    for k, ref in enumerate((m0_ref, m1_ref, m2_ref, m3_ref)):
        block = place_ref[0] ^ k
        for r in range(8):
            part = slice(r * 16, (r + 1) * 16)
            rows = pl.ds(pl.multiple_of(block * 128 + r * 16, 16), 16)
            gradient = gathered_ref[r, k * 16 : (k + 1) * 16, :512].astype(f32)
            new_first, new_second = moments(gradient, ref[part, :512].astype(f32), ref[part, 512:].astype(f32))
            weight_out[rows, :] = (
                weight_ref[rows, :].astype(f32) * (1.0 - learn_rate * decay_rate)
                - learn_rate * new_first / (jnp.sqrt(new_second) + eps_adam)
            ).astype(bf16)


def update(place, *args):
    shard = args[-1]
    return pl.pallas_call(
        update_kernel,
        in_specs=[pl.BlockSpec(memory_space=pltpu.SMEM)] + [pl.BlockSpec(memory_space=pltpu.VMEM)] * len(args),
        out_specs=[pl.BlockSpec(memory_space=pltpu.VMEM)] * 3,
        out_shape=[jax.ShapeDtypeStruct(s, k) for s, k in (((KV, 512), bf16), (shard.shape, f32), (shard.shape, f32))],
        compiler_params=pltpu.CompilerParams(vmem_limit_bytes=32 * 1024 * 1024),
    )(place, *args)


def state_kernel(weight_ref, first_ref, second_ref, out_ref):
    out_ref[:, :, :512] = jnp.broadcast_to(weight_ref[...], (N_GROUP, 16, 512))
    out_ref[:, :, 512:1024] = jnp.broadcast_to(first_ref[...].astype(bf16), (N_GROUP, 16, 512))
    out_ref[:, :, 1024:] = jnp.broadcast_to(second_ref[...].astype(bf16), (N_GROUP, 16, 512))


def body(norm_input, key_grad, positions, norm_gain, key_weight, first_moment, second_moment):
    state = local_call(
        state_kernel, [((N_GROUP, 16, 1536), bf16)], key_weight, first_moment, second_moment, vmem=56
    )[0]
    state = exchange(state, GROUP).reshape(N_GROUP * 16, 1536)
    cosine, sine = rotation(positions)
    send, keys, scale, gain = prepare(norm_input, key_grad, cosine, sine, norm_gain.reshape(D // HEAD, HEAD))
    send, state = lax.optimization_barrier((send, state))

    weights = lax.all_gather(state[:, :512], ("yh", "yl", "z"), axis=0, tiled=True).reshape(2, 4, 8, 128, 512)

    received = exchange(send, GROUP)
    moments = state[:, 512:]
    moments = [moments, *from_others(moments, "yl")]
    received, *moments = lax.optimization_barrier((received, *moments))
    partial = product(received).reshape(N_PLANE, 16, 512)
    pieces = exchange(partial, PLANE)
    piece, square = add_pieces(pieces)

    shards = [
        lax.ppermute(
            piece,
            ("yl", "x", "c", "z"),
            [((y * 8 + i) * 8 + j, ((y ^ k) * 8 + j) * 8 + i) for y in range(4) for i in range(8) for j in range(8)],
        )
        for k in range(4)
    ]
    grad_shard = shards[0]
    late = late_rows(exchange(square, PLANE), shards)
    weights, _ = lax.optimization_barrier((weights, late))
    gathered = exchange(late, GROUP)
    input_grad = backward(keys, weights, norm_input, scale, gain)
    weights, input_grad = lax.optimization_barrier((weights, input_grad))
    at = (lax.axis_index("yh"), 0, lax.axis_index("z"), 0, 0)
    weight = lax.dynamic_slice(weights, at, (1, 4, 1, 128, 512)).reshape(KV, 512)
    place = lax.axis_index("yl").astype(jnp.int32).reshape(1)
    new_weight, new_first, new_second = update(
        place, gathered, weight, *moments, grad_shard, first_moment, second_moment
    )
    return (input_grad, new_weight, new_first, new_second)


def solution(mesh):
    split = Mesh(mesh.devices.reshape(4, 4, 2, 8, 2), ("yl", "x", "c", "z", "yh"))
    placed = (
        P(DP_TENSOR, None),
        P(DP_TENSOR, None),
        P(DP_TENSOR),
        P(),
        P(DP, TENSOR),
        P(DP, TENSOR),
        P(DP, TENSOR),
    )
    return jax.shard_map(
        body,
        mesh=split,
        in_specs=placed,
        out_specs=(P(DP_TENSOR, None), P(None, TENSOR), P(DP, TENSOR), P(DP, TENSOR)),
        check_vma=False,
    )
```

```python
import math

import jax
import jax.numpy as jnp
from jax import lax
from jax.experimental import pallas as pl
from jax.experimental.pallas import tpu as pltpu
from jax.sharding import Mesh
from jax.sharding import PartitionSpec as P

D = 8192
KV_HEADS = 4
HEAD = 128
KV = KV_HEADS * HEAD
DP = ("yl", "x", "c")
TENSOR = ("z", "yh")
DP_TENSOR = DP + TENSOR
GROUP = ("x", "c")
PLANE = ("yl", "z", "yh")
N_GROUP = 8
N_PLANE = 64
WIDE = D // N_GROUP
COLS = WIDE + KV

eps_norm = 1e-05
beta_one = 0.9
beta_two = 0.95
learn_rate = 0.0003
decay_rate = 0.1
eps_adam = 1e-08

bf16 = jnp.bfloat16
f32 = jnp.float32


def exchange(x, axes):
    return lax.all_to_all(x, axes, split_axis=0, concat_axis=0, tiled=True)


def rotation(positions):
    half_width = HEAD // 2
    frequency = 500000.0 ** (-(2.0 * jnp.arange(half_width, dtype=f32)) / HEAD)
    angles = positions.astype(f32)[:, None] * frequency[None, :]
    cosine = jnp.cos(angles)
    sine = jnp.sin(angles)
    return cosine, sine


def prepare_kernel(x_ref, key_ref, cos_ref, sin_ref, gain_ref, send_ref, key_out_ref, scale_ref, gain_out_ref):
    x = x_ref[...].astype(f32)
    scale = lax.rsqrt(jnp.sum(x * x, axis=1, keepdims=True) / D + eps_norm)
    scale_ref[...] = jnp.broadcast_to(scale, scale_ref.shape)
    gain = gain_ref[...].astype(f32)
    gain_out_ref[...] = gain
    for k in range(D // HEAD):
        j, at = divmod(k * HEAD, WIDE)
        part = x_ref[:, k * HEAD : (k + 1) * HEAD].astype(f32)
        send_ref[j, :, at : at + HEAD] = (part * scale * gain[k : k + 1]).astype(bf16)
    cosine = jnp.concatenate([cos_ref[...], cos_ref[...]], axis=1)
    sine = jnp.concatenate([sin_ref[...], -sin_ref[...]], axis=1)
    for h in range(KV_HEADS):
        part = key_ref[:, h * HEAD : (h + 1) * HEAD].astype(f32)
        turned = part * cosine + pltpu.roll(part, HEAD // 2, 1) * sine
        turned = turned.astype(bf16)
        key_out_ref[:, h * HEAD : (h + 1) * HEAD] = turned
        for j in range(N_GROUP):
            send_ref[j, :, WIDE + h * HEAD : WIDE + (h + 1) * HEAD] = turned


def prepare(x, key_grad, cosine, sine, gain):
    tokens = x.shape[0]
    tile = 32
    return pl.pallas_call(
        prepare_kernel,
        grid=(tokens // tile,),
        in_specs=[
            pl.BlockSpec((tile, D), lambda i: (i, 0)),
            pl.BlockSpec((tile, KV), lambda i: (i, 0)),
            pl.BlockSpec((tile, HEAD // 2), lambda i: (i, 0)),
            pl.BlockSpec((tile, HEAD // 2), lambda i: (i, 0)),
            pl.BlockSpec(gain.shape, lambda i: (0, 0)),
        ],
        out_specs=[
            pl.BlockSpec((N_GROUP, tile, COLS), lambda i: (0, i, 0)),
            pl.BlockSpec((tile, KV), lambda i: (i, 0)),
            pl.BlockSpec((tile, HEAD), lambda i: (i, 0)),
            pl.BlockSpec(gain.shape, lambda i: (0, 0)),
        ],
        out_shape=[
            jax.ShapeDtypeStruct((N_GROUP, tokens, COLS), bf16),
            jax.ShapeDtypeStruct((tokens, KV), bf16),
            jax.ShapeDtypeStruct((tokens, HEAD), f32),
            jax.ShapeDtypeStruct(gain.shape, f32),
        ],
        compiler_params=pltpu.CompilerParams(vmem_limit_bytes=56 * 1024 * 1024),
        cost_estimate=pl.CostEstimate(flops=8 * tokens * D, bytes_accessed=6 * 1024 * 1024, transcendentals=0),
    )(x, key_grad, cosine, sine, gain)


def product_kernel(key_ref, normed_ref, out_ref):
    tokens = key_ref.shape[0] * key_ref.shape[1]
    keys = key_ref[...].reshape(tokens, KV)
    normed = normed_ref[...].reshape(tokens, normed_ref.shape[2])
    total = lax.dot_general(keys, normed, (((0,), (0,)), ((), ())), preferred_element_type=f32)
    out_ref[...] = total.astype(bf16).reshape(out_ref.shape)


def product(received):
    count, tokens, _ = received.shape
    half = WIDE // 2
    return pl.pallas_call(
        product_kernel,
        grid=(2,),
        in_specs=[
            pl.BlockSpec((count, tokens, KV), lambda h: (0, 0, WIDE // KV)),
            pl.BlockSpec((count, tokens, half), lambda h: (0, 0, h)),
        ],
        out_specs=pl.BlockSpec((32, 1, 16, half), lambda h: (0, h, 0, 0)),
        out_shape=jax.ShapeDtypeStruct((32, 2, 16, half), bf16),
        compiler_params=pltpu.CompilerParams(vmem_limit_bytes=32 * 1024 * 1024),
        cost_estimate=pl.CostEstimate(
            flops=2 * count * tokens * KV * WIDE, bytes_accessed=4 * 1024 * 1024, transcendentals=0
        ),
    )(received, received)


def backward_kernel(key_ref, weight_ref, x_ref, scale_ref, gain_ref, out_ref, held, cross):
    step = pl.program_id(0)
    deep, width = weight_ref.shape[2], weight_ref.shape[4]

    @pl.when(step == 0)
    def _():
        cross[...] = jnp.zeros_like(cross)

    total = jnp.zeros(cross.shape, f32)
    for z in range(deep):
        for yh in range(2):
            block = (step * deep + z) * 2 + yh
            up = jnp.dot(key_ref[...], weight_ref[yh, :, z].reshape(KV, width), preferred_element_type=f32)
            for k in range(width // HEAD):
                group = block * (width // HEAD) + k
                columns = pl.ds(pl.multiple_of(group * HEAD, HEAD), HEAD)
                inside = slice(k * HEAD, (k + 1) * HEAD)
                weighted = up[:, inside] * gain_ref[pl.ds(group, 1), :]
                held[block, :, inside] = weighted
                total += weighted * x_ref[:, columns].astype(f32)
    cross[...] += total

    @pl.when(step == pl.num_programs(0) - 1)
    def _():
        scale = scale_ref[:, :1]
        inner = scale * scale * (jnp.sum(cross[...], axis=1, keepdims=True) / D)
        for t in range(D // width):
            part = slice(t * width, (t + 1) * width)
            x = x_ref[:, part].astype(f32)
            out_ref[:, part] = (scale * (held[t] - x * inner)).astype(bf16)


def backward(keys, weights, x, scale, gain):
    tokens = x.shape[0]
    width = 512
    deep = 2
    steps = 8 // deep
    whole = lambda a: pl.BlockSpec(a.shape, lambda t: (0, 0))
    return pl.pallas_call(
        backward_kernel,
        grid=(steps,),
        in_specs=[
            whole(keys),
            pl.BlockSpec((2, 4, deep, 128, width), lambda t: (0, 0, t, 0, 0)),
            whole(x),
            whole(scale),
            whole(gain),
        ],
        out_specs=pl.BlockSpec((tokens, D), lambda t: (0, 0)),
        scratch_shapes=[pltpu.VMEM((D // width, tokens, width), f32), pltpu.VMEM((tokens, HEAD), f32)],
        out_shape=jax.ShapeDtypeStruct((tokens, D), bf16),
        compiler_params=pltpu.CompilerParams(vmem_limit_bytes=56 * 1024 * 1024),
        cost_estimate=pl.CostEstimate(
            flops=2 * tokens * KV * D, bytes_accessed=12 * 1024 * 1024, transcendentals=0
        ),
    )(keys, weights, x, scale, gain)


def local_call(kernel, outs, *args, vmem=32):
    return pl.pallas_call(
        kernel,
        out_shape=[jax.ShapeDtypeStruct(shape, kind) for shape, kind in outs],
        compiler_params=pltpu.CompilerParams(vmem_limit_bytes=vmem * 1024 * 1024),
    )(*args)


def from_others(x, axes):
    count = math.prod(lax.axis_size(axis) for axis in axes)
    return [lax.ppermute(x, axes, [(i, i ^ k) for i in range(count)]) for k in range(1, count)]


def add_pieces_kernel(pieces_ref, piece_ref, square_ref):
    piece = jnp.sum(pieces_ref[...].astype(f32), axis=0)
    piece_ref[...] = piece
    square = jnp.sum(jnp.sum(piece * piece, axis=0, keepdims=True), axis=1, keepdims=True)
    square_ref[...] = jnp.broadcast_to(square, square_ref.shape)


def add_pieces(pieces):
    return local_call(add_pieces_kernel, [(pieces.shape[1:], f32), ((N_PLANE, 128), f32)], pieces)


def late_kernel(squares_ref, s0_ref, s1_ref, s2_ref, s3_ref, out_ref):
    for k, ref in enumerate((s0_ref, s1_ref, s2_ref, s3_ref)):
        rows = slice(k * 16, (k + 1) * 16)
        out_ref[:, rows, :512] = jnp.broadcast_to(ref[...].astype(bf16), (N_GROUP, 16, 512))
    rest = jnp.broadcast_to(jnp.sum(squares_ref[...], axis=0, keepdims=True), (64, 128))
    lane = lax.broadcasted_iota(jnp.int32, (64, 128), 1)
    beside = jnp.zeros((64, 128), f32)
    for k in range(3):
        term = rest.astype(bf16).astype(f32)
        rest = rest - term
        beside = jnp.where(lane == k, term, beside)
    out_ref[:, :, 512:] = jnp.broadcast_to(beside.astype(bf16), (N_GROUP, 64, 128))


def late_rows(squares, shards):
    return local_call(late_kernel, [((N_GROUP, 64, 640), bf16)], squares, *shards)[0]


def update_kernel(place_ref, gathered_ref, weight_ref, *refs):
    moment_refs = refs[:N_GROUP]
    shard_ref, first_ref, second_ref, weight_out, first_out, second_out = refs[N_GROUP:]
    terms = jnp.sum(gathered_ref[:, :16, 512:].astype(f32), axis=0)
    total_square = jnp.sum(terms[:1], axis=1, keepdims=True)
    clip_limit = math.sqrt(KV * D)
    clip_factor = jnp.minimum(1.0, clip_limit / (jnp.sqrt(total_square) + 1e-06))

    def moments(gradient, first, second):
        clipped = gradient * clip_factor
        return (
            beta_one * first + (1.0 - beta_one) * clipped,
            beta_two * second + (1.0 - beta_two) * clipped * clipped,
        )

    new_first, new_second = moments(shard_ref[...], first_ref[...], second_ref[...])
    first_out[...] = new_first
    second_out[...] = new_second
    for j, ref in enumerate(moment_refs):
        group = place_ref[1] ^ j
        for k in range(4):
            rows = pl.ds(pl.multiple_of(((place_ref[0] ^ k) * N_GROUP + group) * 16, 16), 16)
            gradient = gathered_ref[group, k * 16 : (k + 1) * 16, :512].astype(f32)
            new_first, new_second = moments(gradient, ref[k, :, :512].astype(f32), ref[k, :, 512:].astype(f32))
            weight_out[rows, :] = (
                weight_ref[rows, :].astype(f32) * (1.0 - learn_rate * decay_rate)
                - learn_rate * new_first / (jnp.sqrt(new_second) + eps_adam)
            ).astype(bf16)


def update(place, *args):
    shard = args[-1]
    return pl.pallas_call(
        update_kernel,
        in_specs=[pl.BlockSpec(memory_space=pltpu.SMEM)] + [pl.BlockSpec(memory_space=pltpu.VMEM)] * len(args),
        out_specs=[pl.BlockSpec(memory_space=pltpu.VMEM)] * 3,
        out_shape=[jax.ShapeDtypeStruct(s, k) for s, k in (((KV, 512), bf16), (shard.shape, f32), (shard.shape, f32))],
        compiler_params=pltpu.CompilerParams(vmem_limit_bytes=32 * 1024 * 1024),
    )(place, *args)


def stack_kernel(*refs):
    for k, ref in enumerate(refs[:-1]):
        refs[-1][k] = ref[...]


def round_kernel(first_ref, second_ref, out_ref):
    out_ref[:, :512] = first_ref[...].astype(bf16)
    out_ref[:, 512:] = second_ref[...].astype(bf16)


def body(norm_input, key_grad, positions, norm_gain, key_weight, first_moment, second_moment):
    weights = exchange(jnp.broadcast_to(key_weight, (N_GROUP, *key_weight.shape)), GROUP)
    cosine, sine = rotation(positions)
    send, keys, scale, gain = prepare(norm_input, key_grad, cosine, sine, norm_gain.reshape(D // HEAD, HEAD))
    send, weights = lax.optimization_barrier((send, weights))

    weights = lax.all_gather(weights.reshape(128, 512), ("yh", "yl", "z"), axis=0, tiled=True)
    weights = weights.reshape(2, 4, 8, 128, 512)

    received = exchange(send, GROUP)
    moments = local_call(round_kernel, [((16, 1024), bf16)], first_moment, second_moment, vmem=56)[0]
    moments, _ = lax.optimization_barrier((moments, send))
    moments = local_call(stack_kernel, [((4, 16, 1024), bf16)], moments, *from_others(moments, ("yl",)))[0]
    received, moments = lax.optimization_barrier((received, moments))
    partial = product(received).reshape(N_PLANE, 16, 512)
    partial, moments = lax.optimization_barrier((partial, moments))
    pieces = exchange(partial, PLANE)
    moments = [moments, *from_others(moments, GROUP)]
    pieces, *moments = lax.optimization_barrier((pieces, *moments))
    piece, square = add_pieces(pieces)

    swap = [(i * 8 + k, k * 8 + i) for i in range(8) for k in range(8)]
    grad_shard = lax.ppermute(piece, ("x", "c", "z"), swap)
    shards = [grad_shard, *from_others(grad_shard, ("yl",))]
    late = late_rows(exchange(square, PLANE), shards)
    weights, _ = lax.optimization_barrier((weights, late))
    gathered = exchange(late, GROUP)
    input_grad = backward(keys, weights, norm_input, scale, gain)
    weights, input_grad = lax.optimization_barrier((weights, input_grad))
    at = (lax.axis_index("yh"), 0, lax.axis_index("z"), 0, 0)
    weight = lax.dynamic_slice(weights, at, (1, 4, 1, 128, 512)).reshape(KV, 512)
    place = jnp.stack([lax.axis_index("yl"), lax.axis_index(GROUP)]).astype(jnp.int32)
    new_weight, new_first, new_second = update(
        place, gathered, weight, *moments, grad_shard, first_moment, second_moment
    )
    return (input_grad, new_weight, new_first, new_second)


def solution(mesh):
    split = Mesh(mesh.devices.reshape(4, 4, 2, 8, 2), ("yl", "x", "c", "z", "yh"))
    placed = (
        P(DP_TENSOR, None),
        P(DP_TENSOR, None),
        P(DP_TENSOR),
        P(),
        P(DP, TENSOR),
        P(DP, TENSOR),
        P(DP, TENSOR),
    )
    return jax.shard_map(
        body,
        mesh=split,
        in_specs=placed,
        out_specs=(P(DP_TENSOR, None), P(None, TENSOR), P(DP, TENSOR), P(DP, TENSOR)),
        check_vma=False,
    )
```

```python
import math

import jax
import jax.numpy as jnp
from jax import lax
from jax.experimental import pallas as pl
from jax.experimental.pallas import tpu as pltpu
from jax.sharding import Mesh
from jax.sharding import PartitionSpec as P

D = 8192
KV_HEADS = 4
HEAD = 128
KV = KV_HEADS * HEAD
DP = ("yl", "x", "c")
TENSOR = ("z", "yh")
DP_TENSOR = DP + TENSOR
GROUP = ("x", "c")
PLANE = ("yl", "z", "yh")
N_GROUP = 8
N_PLANE = 64
WIDE = D // N_GROUP
COLS = WIDE + KV

eps_norm = 1e-05
beta_one = 0.9
beta_two = 0.95
learn_rate = 0.0003
decay_rate = 0.1
eps_adam = 1e-08

bf16 = jnp.bfloat16
f32 = jnp.float32


def exchange(x, axes):
    return lax.all_to_all(x, axes, split_axis=0, concat_axis=0, tiled=True)


def rotation(positions):
    half_width = HEAD // 2
    frequency = 500000.0 ** (-(2.0 * jnp.arange(half_width, dtype=f32)) / HEAD)
    angles = positions.astype(f32)[:, None] * frequency[None, :]
    cosine = jnp.cos(angles)
    sine = jnp.sin(angles)
    return cosine, sine


def prepare_kernel(x_ref, key_ref, cos_ref, sin_ref, gain_ref, send_ref, key_out_ref, scale_ref, gain_out_ref):
    x = x_ref[...].astype(f32)
    scale = lax.rsqrt(jnp.sum(x * x, axis=1, keepdims=True) / D + eps_norm)
    scale_ref[...] = jnp.broadcast_to(scale, scale_ref.shape)
    gain = gain_ref[...].astype(f32)
    gain_out_ref[...] = gain
    for k in range(D // HEAD):
        j, at = divmod(k * HEAD, WIDE)
        part = x_ref[:, k * HEAD : (k + 1) * HEAD].astype(f32)
        send_ref[j, :, at : at + HEAD] = (part * scale * gain[k : k + 1]).astype(bf16)
    cosine = jnp.concatenate([cos_ref[...], cos_ref[...]], axis=1)
    sine = jnp.concatenate([sin_ref[...], -sin_ref[...]], axis=1)
    for h in range(KV_HEADS):
        part = key_ref[:, h * HEAD : (h + 1) * HEAD].astype(f32)
        turned = part * cosine + pltpu.roll(part, HEAD // 2, 1) * sine
        turned = turned.astype(bf16)
        key_out_ref[:, h * HEAD : (h + 1) * HEAD] = turned
        for j in range(N_GROUP):
            send_ref[j, :, WIDE + h * HEAD : WIDE + (h + 1) * HEAD] = turned


def prepare(x, key_grad, cosine, sine, gain):
    tokens = x.shape[0]
    tile = 32
    return pl.pallas_call(
        prepare_kernel,
        grid=(tokens // tile,),
        in_specs=[
            pl.BlockSpec((tile, D), lambda i: (i, 0)),
            pl.BlockSpec((tile, KV), lambda i: (i, 0)),
            pl.BlockSpec((tile, HEAD // 2), lambda i: (i, 0)),
            pl.BlockSpec((tile, HEAD // 2), lambda i: (i, 0)),
            pl.BlockSpec(gain.shape, lambda i: (0, 0)),
        ],
        out_specs=[
            pl.BlockSpec((N_GROUP, tile, COLS), lambda i: (0, i, 0)),
            pl.BlockSpec((tile, KV), lambda i: (i, 0)),
            pl.BlockSpec((tile, HEAD), lambda i: (i, 0)),
            pl.BlockSpec(gain.shape, lambda i: (0, 0)),
        ],
        out_shape=[
            jax.ShapeDtypeStruct((N_GROUP, tokens, COLS), bf16),
            jax.ShapeDtypeStruct((tokens, KV), bf16),
            jax.ShapeDtypeStruct((tokens, HEAD), f32),
            jax.ShapeDtypeStruct(gain.shape, f32),
        ],
        compiler_params=pltpu.CompilerParams(vmem_limit_bytes=56 * 1024 * 1024),
        cost_estimate=pl.CostEstimate(flops=8 * tokens * D, bytes_accessed=6 * 1024 * 1024, transcendentals=0),
    )(x, key_grad, cosine, sine, gain)


def product_kernel(key_ref, normed_ref, out_ref):
    tokens = key_ref.shape[0] * key_ref.shape[1]
    keys = key_ref[...].reshape(tokens, KV)
    normed = normed_ref[...].reshape(tokens, normed_ref.shape[2])
    total = lax.dot_general(keys, normed, (((0,), (0,)), ((), ())), preferred_element_type=f32)
    out_ref[...] = total.astype(bf16).reshape(out_ref.shape)


def product(received):
    count, tokens, _ = received.shape
    half = WIDE // 2
    return pl.pallas_call(
        product_kernel,
        grid=(2,),
        in_specs=[
            pl.BlockSpec((count, tokens, KV), lambda h: (0, 0, WIDE // KV)),
            pl.BlockSpec((count, tokens, half), lambda h: (0, 0, h)),
        ],
        out_specs=pl.BlockSpec((32, 1, 16, half), lambda h: (0, h, 0, 0)),
        out_shape=jax.ShapeDtypeStruct((32, 2, 16, half), bf16),
        compiler_params=pltpu.CompilerParams(vmem_limit_bytes=32 * 1024 * 1024),
        cost_estimate=pl.CostEstimate(
            flops=2 * count * tokens * KV * WIDE, bytes_accessed=4 * 1024 * 1024, transcendentals=0
        ),
    )(received, received)


def backward_kernel(key_ref, weight_ref, x_ref, scale_ref, gain_ref, out_ref, held, cross):
    step = pl.program_id(0)
    deep, width = weight_ref.shape[2], weight_ref.shape[4]

    @pl.when(step == 0)
    def _():
        cross[...] = jnp.zeros_like(cross)

    total = jnp.zeros(cross.shape, f32)
    for z in range(deep):
        for yh in range(2):
            block = (step * deep + z) * 2 + yh
            up = jnp.dot(key_ref[...], weight_ref[yh, :, z].reshape(KV, width), preferred_element_type=f32)
            for k in range(width // HEAD):
                group = block * (width // HEAD) + k
                columns = pl.ds(pl.multiple_of(group * HEAD, HEAD), HEAD)
                inside = slice(k * HEAD, (k + 1) * HEAD)
                weighted = up[:, inside] * gain_ref[pl.ds(group, 1), :]
                held[block, :, inside] = weighted
                total += weighted * x_ref[:, columns].astype(f32)
    cross[...] += total

    @pl.when(step == pl.num_programs(0) - 1)
    def _():
        scale = scale_ref[:, :1]
        inner = scale * scale * (jnp.sum(cross[...], axis=1, keepdims=True) / D)
        for t in range(D // width):
            part = slice(t * width, (t + 1) * width)
            x = x_ref[:, part].astype(f32)
            out_ref[:, part] = (scale * (held[t] - x * inner)).astype(bf16)


def backward(keys, weights, x, scale, gain):
    tokens = x.shape[0]
    width = 512
    deep = 2
    steps = 8 // deep
    whole = lambda a: pl.BlockSpec(a.shape, lambda t: (0, 0))
    return pl.pallas_call(
        backward_kernel,
        grid=(steps,),
        in_specs=[
            whole(keys),
            pl.BlockSpec((2, 4, deep, 128, width), lambda t: (0, 0, t, 0, 0)),
            whole(x),
            whole(scale),
            whole(gain),
        ],
        out_specs=pl.BlockSpec((tokens, D), lambda t: (0, 0)),
        scratch_shapes=[pltpu.VMEM((D // width, tokens, width), f32), pltpu.VMEM((tokens, HEAD), f32)],
        out_shape=jax.ShapeDtypeStruct((tokens, D), bf16),
        compiler_params=pltpu.CompilerParams(vmem_limit_bytes=56 * 1024 * 1024),
        cost_estimate=pl.CostEstimate(
            flops=2 * tokens * KV * D, bytes_accessed=12 * 1024 * 1024, transcendentals=0
        ),
    )(keys, weights, x, scale, gain)


def local_call(kernel, outs, *args, vmem=32):
    return pl.pallas_call(
        kernel,
        out_shape=[jax.ShapeDtypeStruct(shape, kind) for shape, kind in outs],
        compiler_params=pltpu.CompilerParams(vmem_limit_bytes=vmem * 1024 * 1024),
    )(*args)


def from_others(x, axis):
    count = lax.axis_size(axis)
    return [lax.ppermute(x, axis, [(i, i ^ k) for i in range(count)]) for k in range(1, count)]


def add_pieces_kernel(pieces_ref, piece_ref, square_ref):
    piece = jnp.sum(pieces_ref[...].astype(f32), axis=0)
    piece_ref[...] = piece
    square = jnp.sum(jnp.sum(piece * piece, axis=0, keepdims=True), axis=1, keepdims=True)
    square_ref[...] = jnp.broadcast_to(square, square_ref.shape)


def add_pieces(pieces):
    return local_call(add_pieces_kernel, [(pieces.shape[1:], f32), ((N_PLANE, 128), f32)], pieces)


def late_kernel(squares_ref, s0_ref, s1_ref, s2_ref, s3_ref, out_ref):
    for k, ref in enumerate((s0_ref, s1_ref, s2_ref, s3_ref)):
        rows = slice(k * 16, (k + 1) * 16)
        out_ref[:, rows, :512] = jnp.broadcast_to(ref[...].astype(bf16), (N_GROUP, 16, 512))
    rest = jnp.broadcast_to(jnp.sum(squares_ref[...], axis=0, keepdims=True), (64, 128))
    lane = lax.broadcasted_iota(jnp.int32, (64, 128), 1)
    beside = jnp.zeros((64, 128), f32)
    for k in range(3):
        term = rest.astype(bf16).astype(f32)
        rest = rest - term
        beside = jnp.where(lane == k, term, beside)
    out_ref[:, :, 512:] = jnp.broadcast_to(beside.astype(bf16), (N_GROUP, 64, 128))


def late_rows(squares, shards):
    return local_call(late_kernel, [((N_GROUP, 64, 640), bf16)], squares, *shards)[0]


def update_kernel(
    place_ref, gathered_ref, weight_ref, m0_ref, m1_ref, m2_ref, m3_ref, shard_ref, first_ref, second_ref,
    weight_out, first_out, second_out,
):
    terms = jnp.sum(gathered_ref[:, :16, 512:].astype(f32), axis=0)
    total_square = jnp.sum(terms[:1], axis=1, keepdims=True)
    clip_limit = math.sqrt(KV * D)
    clip_factor = jnp.minimum(1.0, clip_limit / (jnp.sqrt(total_square) + 1e-06))

    def moments(gradient, first, second):
        clipped = gradient * clip_factor
        return (
            beta_one * first + (1.0 - beta_one) * clipped,
            beta_two * second + (1.0 - beta_two) * clipped * clipped,
        )

    new_first, new_second = moments(shard_ref[...], first_ref[...], second_ref[...])
    first_out[...] = new_first
    second_out[...] = new_second
    for k, ref in enumerate((m0_ref, m1_ref, m2_ref, m3_ref)):
        block = place_ref[0] ^ k
        for r in range(8):
            part = slice(r * 16, (r + 1) * 16)
            rows = pl.ds(pl.multiple_of(block * 128 + r * 16, 16), 16)
            gradient = gathered_ref[r, k * 16 : (k + 1) * 16, :512].astype(f32)
            new_first, new_second = moments(gradient, ref[part, :512].astype(f32), ref[part, 512:].astype(f32))
            weight_out[rows, :] = (
                weight_ref[rows, :].astype(f32) * (1.0 - learn_rate * decay_rate)
                - learn_rate * new_first / (jnp.sqrt(new_second) + eps_adam)
            ).astype(bf16)


def update(place, *args):
    shard = args[-1]
    return pl.pallas_call(
        update_kernel,
        in_specs=[pl.BlockSpec(memory_space=pltpu.SMEM)] + [pl.BlockSpec(memory_space=pltpu.VMEM)] * len(args),
        out_specs=[pl.BlockSpec(memory_space=pltpu.VMEM)] * 3,
        out_shape=[jax.ShapeDtypeStruct(s, k) for s, k in (((KV, 512), bf16), (shard.shape, f32), (shard.shape, f32))],
        compiler_params=pltpu.CompilerParams(vmem_limit_bytes=32 * 1024 * 1024),
    )(place, *args)


def state_kernel(weight_ref, first_ref, second_ref, out_ref):
    out_ref[:, :, :512] = jnp.broadcast_to(weight_ref[...], (N_GROUP, 16, 512))
    out_ref[:, :, 512:1024] = jnp.broadcast_to(first_ref[...].astype(bf16), (N_GROUP, 16, 512))
    out_ref[:, :, 1024:] = jnp.broadcast_to(second_ref[...].astype(bf16), (N_GROUP, 16, 512))


def body(norm_input, key_grad, positions, norm_gain, key_weight, first_moment, second_moment):
    state = local_call(
        state_kernel, [((N_GROUP, 16, 1536), bf16)], key_weight, first_moment, second_moment, vmem=56
    )[0]
    state = exchange(state, GROUP).reshape(N_GROUP * 16, 1536)
    cosine, sine = rotation(positions)
    send, keys, scale, gain = prepare(norm_input, key_grad, cosine, sine, norm_gain.reshape(D // HEAD, HEAD))
    send, state = lax.optimization_barrier((send, state))

    weights = lax.all_gather(state[:, :512], ("yh", "yl", "z"), axis=0, tiled=True).reshape(2, 4, 8, 128, 512)

    received = exchange(send, GROUP)
    moments = state[:, 512:]
    moments = [moments, *from_others(moments, "yl")]
    received, *moments = lax.optimization_barrier((received, *moments))
    partial = product(received).reshape(N_PLANE, 16, 512)
    pieces = exchange(partial, PLANE)
    piece, square = add_pieces(pieces)

    swap = [(i * 8 + k, k * 8 + i) for i in range(8) for k in range(8)]
    grad_shard = lax.ppermute(piece, ("x", "c", "z"), swap)
    shards = [grad_shard, *from_others(grad_shard, "yl")]
    late = late_rows(exchange(square, PLANE), shards)
    weights, _ = lax.optimization_barrier((weights, late))
    gathered = exchange(late, GROUP)
    input_grad = backward(keys, weights, norm_input, scale, gain)
    weights, input_grad = lax.optimization_barrier((weights, input_grad))
    at = (lax.axis_index("yh"), 0, lax.axis_index("z"), 0, 0)
    weight = lax.dynamic_slice(weights, at, (1, 4, 1, 128, 512)).reshape(KV, 512)
    place = lax.axis_index("yl").astype(jnp.int32).reshape(1)
    new_weight, new_first, new_second = update(
        place, gathered, weight, *moments, grad_shard, first_moment, second_moment
    )
    return (input_grad, new_weight, new_first, new_second)


def solution(mesh):
    split = Mesh(mesh.devices.reshape(4, 4, 2, 8, 2), ("yl", "x", "c", "z", "yh"))
    placed = (
        P(DP_TENSOR, None),
        P(DP_TENSOR, None),
        P(DP_TENSOR),
        P(),
        P(DP, TENSOR),
        P(DP, TENSOR),
        P(DP, TENSOR),
    )
    return jax.shard_map(
        body,
        mesh=split,
        in_specs=placed,
        out_specs=(P(DP_TENSOR, None), P(None, TENSOR), P(DP, TENSOR), P(DP, TENSOR)),
        check_vma=False,
    )
```

```python
import math

import jax
import jax.numpy as jnp
from jax import lax
from jax.experimental import pallas as pl
from jax.experimental.pallas import tpu as pltpu
from jax.sharding import Mesh
from jax.sharding import PartitionSpec as P

D = 8192
KV_HEADS = 4
HEAD = 128
KV = KV_HEADS * HEAD
DP = ("yl", "x", "c")
TENSOR = ("z", "yh")
DP_TENSOR = DP + TENSOR
GROUP = ("x", "c")
PLANE = ("yl", "z", "yh")
N_GROUP = 8
N_PLANE = 64
WIDE = D // N_GROUP
COLS = WIDE + KV

eps_norm = 1e-05
beta_one = 0.9
beta_two = 0.95
learn_rate = 0.0003
decay_rate = 0.1
eps_adam = 1e-08

bf16 = jnp.bfloat16
f32 = jnp.float32


def exchange(x, axes):
    return lax.all_to_all(x, axes, split_axis=0, concat_axis=0, tiled=True)


def rotation(positions):
    half_width = HEAD // 2
    frequency = 500000.0 ** (-(2.0 * jnp.arange(half_width, dtype=f32)) / HEAD)
    angles = positions.astype(f32)[:, None] * frequency[None, :]
    cosine = jnp.cos(angles)
    sine = jnp.sin(angles)
    return cosine, sine


def prepare_kernel(x_ref, key_ref, cos_ref, sin_ref, gain_ref, send_ref, key_out_ref, scale_ref, gain_out_ref):
    x = x_ref[...].astype(f32)
    scale = lax.rsqrt(jnp.sum(x * x, axis=1, keepdims=True) / D + eps_norm)
    scale_ref[...] = jnp.broadcast_to(scale, scale_ref.shape)
    gain = gain_ref[...].astype(f32)
    gain_out_ref[...] = gain
    for k in range(D // HEAD):
        j, at = divmod(k * HEAD, WIDE)
        part = x_ref[:, k * HEAD : (k + 1) * HEAD].astype(f32)
        send_ref[j, :, at : at + HEAD] = (part * scale * gain[k : k + 1]).astype(bf16)
    cosine = jnp.concatenate([cos_ref[...], cos_ref[...]], axis=1)
    sine = jnp.concatenate([sin_ref[...], -sin_ref[...]], axis=1)
    for h in range(KV_HEADS):
        part = key_ref[:, h * HEAD : (h + 1) * HEAD].astype(f32)
        turned = part * cosine + pltpu.roll(part, HEAD // 2, 1) * sine
        turned = turned.astype(bf16)
        key_out_ref[:, h * HEAD : (h + 1) * HEAD] = turned
        for j in range(N_GROUP):
            send_ref[j, :, WIDE + h * HEAD : WIDE + (h + 1) * HEAD] = turned


def prepare(x, key_grad, cosine, sine, gain):
    tokens = x.shape[0]
    tile = 32
    return pl.pallas_call(
        prepare_kernel,
        grid=(tokens // tile,),
        in_specs=[
            pl.BlockSpec((tile, D), lambda i: (i, 0)),
            pl.BlockSpec((tile, KV), lambda i: (i, 0)),
            pl.BlockSpec((tile, HEAD // 2), lambda i: (i, 0)),
            pl.BlockSpec((tile, HEAD // 2), lambda i: (i, 0)),
            pl.BlockSpec(gain.shape, lambda i: (0, 0)),
        ],
        out_specs=[
            pl.BlockSpec((N_GROUP, tile, COLS), lambda i: (0, i, 0)),
            pl.BlockSpec((tile, KV), lambda i: (i, 0)),
            pl.BlockSpec((tile, HEAD), lambda i: (i, 0)),
            pl.BlockSpec(gain.shape, lambda i: (0, 0)),
        ],
        out_shape=[
            jax.ShapeDtypeStruct((N_GROUP, tokens, COLS), bf16),
            jax.ShapeDtypeStruct((tokens, KV), bf16),
            jax.ShapeDtypeStruct((tokens, HEAD), f32),
            jax.ShapeDtypeStruct(gain.shape, f32),
        ],
        compiler_params=pltpu.CompilerParams(vmem_limit_bytes=56 * 1024 * 1024),
        cost_estimate=pl.CostEstimate(flops=8 * tokens * D, bytes_accessed=6 * 1024 * 1024, transcendentals=0),
    )(x, key_grad, cosine, sine, gain)


def product_kernel(key_ref, normed_ref, out_ref):
    tokens = key_ref.shape[0] * key_ref.shape[1]
    keys = key_ref[...].reshape(tokens, KV)
    normed = normed_ref[...].reshape(tokens, normed_ref.shape[2])
    total = lax.dot_general(keys, normed, (((0,), (0,)), ((), ())), preferred_element_type=f32)
    out_ref[...] = total.astype(bf16).reshape(out_ref.shape)


def product(received):
    count, tokens, _ = received.shape
    half = WIDE // 2
    return pl.pallas_call(
        product_kernel,
        grid=(2,),
        in_specs=[
            pl.BlockSpec((count, tokens, KV), lambda h: (0, 0, WIDE // KV)),
            pl.BlockSpec((count, tokens, half), lambda h: (0, 0, h)),
        ],
        out_specs=pl.BlockSpec((32, 1, 16, half), lambda h: (0, h, 0, 0)),
        out_shape=jax.ShapeDtypeStruct((32, 2, 16, half), bf16),
        compiler_params=pltpu.CompilerParams(vmem_limit_bytes=32 * 1024 * 1024),
        cost_estimate=pl.CostEstimate(
            flops=2 * count * tokens * KV * WIDE, bytes_accessed=4 * 1024 * 1024, transcendentals=0
        ),
    )(received, received)


def backward_kernel(key_ref, weight_ref, x_ref, scale_ref, gain_ref, out_ref, held, cross):
    step = pl.program_id(0)
    deep, width = weight_ref.shape[0], weight_ref.shape[4]

    @pl.when(step == 0)
    def _():
        cross[...] = jnp.zeros_like(cross)

    total = jnp.zeros(cross.shape, f32)
    for z in range(deep):
        for yh in range(2):
            block = (step * deep + z) * 2 + yh
            up = jnp.dot(key_ref[...], weight_ref[z, yh].reshape(KV, width), preferred_element_type=f32)
            for k in range(width // HEAD):
                group = block * (width // HEAD) + k
                columns = pl.ds(pl.multiple_of(group * HEAD, HEAD), HEAD)
                inside = slice(k * HEAD, (k + 1) * HEAD)
                weighted = up[:, inside] * gain_ref[pl.ds(group, 1), :]
                held[block, :, inside] = weighted
                total += weighted * x_ref[:, columns].astype(f32)
    cross[...] += total

    @pl.when(step == pl.num_programs(0) - 1)
    def _():
        scale = scale_ref[:, :1]
        inner = scale * scale * (jnp.sum(cross[...], axis=1, keepdims=True) / D)
        for t in range(D // width):
            part = slice(t * width, (t + 1) * width)
            x = x_ref[:, part].astype(f32)
            out_ref[:, part] = (scale * (held[t] - x * inner)).astype(bf16)


def backward(keys, weights, x, scale, gain):
    tokens = x.shape[0]
    width = 512
    deep = 2
    steps = 8 // deep
    whole = lambda a: pl.BlockSpec(a.shape, lambda t: (0, 0))
    return pl.pallas_call(
        backward_kernel,
        grid=(steps,),
        in_specs=[
            whole(keys),
            pl.BlockSpec((deep, 2, 4, 128, width), lambda t: (t, 0, 0, 0, 0)),
            whole(x),
            whole(scale),
            whole(gain),
        ],
        out_specs=pl.BlockSpec((tokens, D), lambda t: (0, 0)),
        scratch_shapes=[pltpu.VMEM((D // width, tokens, width), f32), pltpu.VMEM((tokens, HEAD), f32)],
        out_shape=jax.ShapeDtypeStruct((tokens, D), bf16),
        compiler_params=pltpu.CompilerParams(vmem_limit_bytes=56 * 1024 * 1024),
        cost_estimate=pl.CostEstimate(
            flops=2 * tokens * KV * D, bytes_accessed=12 * 1024 * 1024, transcendentals=0
        ),
    )(keys, weights, x, scale, gain)


def local_call(kernel, outs, *args, vmem=32):
    return pl.pallas_call(
        kernel,
        out_shape=[jax.ShapeDtypeStruct(shape, kind) for shape, kind in outs],
        compiler_params=pltpu.CompilerParams(vmem_limit_bytes=vmem * 1024 * 1024),
    )(*args)


def from_others(x, axis):
    count = lax.axis_size(axis)
    return [lax.ppermute(x, axis, [(i, i ^ k) for i in range(count)]) for k in range(1, count)]


def add_pieces_kernel(pieces_ref, piece_ref, square_ref):
    piece = jnp.sum(pieces_ref[...].astype(f32), axis=0)
    piece_ref[...] = piece
    square = jnp.sum(jnp.sum(piece * piece, axis=0, keepdims=True), axis=1, keepdims=True)
    square_ref[...] = jnp.broadcast_to(square, square_ref.shape)


def add_pieces(pieces):
    return local_call(add_pieces_kernel, [(pieces.shape[1:], f32), ((N_PLANE, 128), f32)], pieces)


def late_kernel(squares_ref, s0_ref, s1_ref, s2_ref, s3_ref, out_ref):
    for k, ref in enumerate((s0_ref, s1_ref, s2_ref, s3_ref)):
        rows = slice(k * 16, (k + 1) * 16)
        out_ref[:, rows, :512] = jnp.broadcast_to(ref[...].astype(bf16), (N_GROUP, 16, 512))
    rest = jnp.broadcast_to(jnp.sum(squares_ref[...], axis=0, keepdims=True), (64, 128))
    lane = lax.broadcasted_iota(jnp.int32, (64, 128), 1)
    beside = jnp.zeros((64, 128), f32)
    for k in range(3):
        term = rest.astype(bf16).astype(f32)
        rest = rest - term
        beside = jnp.where(lane == k, term, beside)
    out_ref[:, :, 512:] = jnp.broadcast_to(beside.astype(bf16), (N_GROUP, 64, 128))


def late_rows(squares, shards):
    return local_call(late_kernel, [((N_GROUP, 64, 640), bf16)], squares, *shards)[0]


def update_kernel(
    place_ref, gathered_ref, weight_ref, m0_ref, m1_ref, m2_ref, m3_ref, shard_ref, first_ref, second_ref,
    weight_out, first_out, second_out,
):
    terms = jnp.sum(gathered_ref[:, :16, 512:].astype(f32), axis=0)
    total_square = jnp.sum(terms[:1], axis=1, keepdims=True)
    clip_limit = math.sqrt(KV * D)
    clip_factor = jnp.minimum(1.0, clip_limit / (jnp.sqrt(total_square) + 1e-06))

    def moments(gradient, first, second):
        clipped = gradient * clip_factor
        return (
            beta_one * first + (1.0 - beta_one) * clipped,
            beta_two * second + (1.0 - beta_two) * clipped * clipped,
        )

    new_first, new_second = moments(shard_ref[...], first_ref[...], second_ref[...])
    first_out[...] = new_first
    second_out[...] = new_second
    for k, ref in enumerate((m0_ref, m1_ref, m2_ref, m3_ref)):
        block = place_ref[0] ^ k
        for r in range(8):
            part = slice(r * 16, (r + 1) * 16)
            rows = pl.ds(pl.multiple_of(block * 128 + r * 16, 16), 16)
            gradient = gathered_ref[r, k * 16 : (k + 1) * 16, :512].astype(f32)
            new_first, new_second = moments(gradient, ref[part, :512].astype(f32), ref[part, 512:].astype(f32))
            weight_out[rows, :] = (
                weight_ref[rows, :].astype(f32) * (1.0 - learn_rate * decay_rate)
                - learn_rate * new_first / (jnp.sqrt(new_second) + eps_adam)
            ).astype(bf16)


def update(place, *args):
    shard = args[-1]
    return pl.pallas_call(
        update_kernel,
        in_specs=[pl.BlockSpec(memory_space=pltpu.SMEM)] + [pl.BlockSpec(memory_space=pltpu.VMEM)] * len(args),
        out_specs=[pl.BlockSpec(memory_space=pltpu.VMEM)] * 3,
        out_shape=[jax.ShapeDtypeStruct(s, k) for s, k in (((KV, 512), bf16), (shard.shape, f32), (shard.shape, f32))],
        compiler_params=pltpu.CompilerParams(vmem_limit_bytes=32 * 1024 * 1024),
    )(place, *args)


def state_kernel(weight_ref, first_ref, second_ref, out_ref):
    out_ref[:, :, :512] = jnp.broadcast_to(weight_ref[...], (N_GROUP, 16, 512))
    out_ref[:, :, 512:1024] = jnp.broadcast_to(first_ref[...].astype(bf16), (N_GROUP, 16, 512))
    out_ref[:, :, 1024:] = jnp.broadcast_to(second_ref[...].astype(bf16), (N_GROUP, 16, 512))


def body(norm_input, key_grad, positions, norm_gain, key_weight, first_moment, second_moment):
    state = local_call(
        state_kernel, [((N_GROUP, 16, 1536), bf16)], key_weight, first_moment, second_moment, vmem=56
    )[0]
    state = exchange(state, GROUP).reshape(N_GROUP * 16, 1536)
    cosine, sine = rotation(positions)
    send, keys, scale, gain = prepare(norm_input, key_grad, cosine, sine, norm_gain.reshape(D // HEAD, HEAD))
    send, state = lax.optimization_barrier((send, state))

    weights = lax.all_gather(state[:, :512], ("z", "yh", "yl"), axis=0, tiled=True).reshape(8, 2, 4, 128, 512)

    received = exchange(send, GROUP)
    moments = state[:, 512:]
    moments = [moments, *from_others(moments, "yl")]
    received, *moments = lax.optimization_barrier((received, *moments))
    partial = product(received).reshape(N_PLANE, 16, 512)
    pieces = exchange(partial, PLANE)
    piece, square = add_pieces(pieces)

    swap = [(i * 8 + k, k * 8 + i) for i in range(8) for k in range(8)]
    grad_shard = lax.ppermute(piece, ("x", "c", "z"), swap)
    shards = [grad_shard, *from_others(grad_shard, "yl")]
    late = late_rows(exchange(square, PLANE), shards)
    weights, _ = lax.optimization_barrier((weights, late))
    gathered = exchange(late, GROUP)
    input_grad = backward(keys, weights, norm_input, scale, gain)
    weights, input_grad = lax.optimization_barrier((weights, input_grad))
    at = (lax.axis_index("z"), lax.axis_index("yh"), 0, 0, 0)
    weight = lax.dynamic_slice(weights, at, (1, 1, 4, 128, 512)).reshape(KV, 512)
    place = lax.axis_index("yl").astype(jnp.int32).reshape(1)
    new_weight, new_first, new_second = update(
        place, gathered, weight, *moments, grad_shard, first_moment, second_moment
    )
    return (input_grad, new_weight, new_first, new_second)


def solution(mesh):
    split = Mesh(mesh.devices.reshape(4, 4, 2, 8, 2), ("yl", "x", "c", "z", "yh"))
    placed = (
        P(DP_TENSOR, None),
        P(DP_TENSOR, None),
        P(DP_TENSOR),
        P(),
        P(DP, TENSOR),
        P(DP, TENSOR),
        P(DP, TENSOR),
    )
    return jax.shard_map(
        body,
        mesh=split,
        in_specs=placed,
        out_specs=(P(DP_TENSOR, None), P(None, TENSOR), P(DP, TENSOR), P(DP, TENSOR)),
        check_vma=False,
    )
```
